512 devices in a mesh: pipe: 16 (over z_hi, x), tensor: 32 (over z_lo, y, core).
Axes of the slice: x: 4, y: 4, z: 16 (z_hi: 4, z_lo: 4; z = z_hi * 4 + z_lo), core: 2. Of those that a mesh axis runs over, the one named last changes fastest.
Arguments:
- hidden: bfloat16 [512, 8192], P('pipe'), may hold values from -6 to 6
- kv_weight: bfloat16 [16, 2048, 8192], P('pipe', 'tensor'), may hold values from -0.0625 to 0.0625
- queries: bfloat16 [16, 512, 8192], P('pipe', None, 'tensor'), may hold values from -5 to 5
- out_grads: bfloat16 [16, 512, 8192], P('pipe', None, 'tensor'), may hold values from -384 to 384
- cache: bfloat16 [16, 2, 32768, 128], P('pipe', None, 'tensor'), may hold values from -5 to 5
- prefix_len: int32 [512], replicated, may hold values from 512 to 4096, as said below
- doc_start: int32 [512], replicated, may hold values from 0 to 511, as said below
Outputs:
- hidden_grads: float32 [512, 8192], P('pipe', 'tensor')
- weight_grads: float32 [16, 2048, 8192], P('pipe', 'tensor')
The draws below stay inside these ranges and needn't reach their ends.
Inputs may be any that keep to these rules, and one draw needn't show every extreme that they name: Row r sees the first prefix_len[r] cached positions; some row sees all 4096. doc_start[0] = 0, for r > 0 doc_start[r] is either doc_start[r-1] or r, and the last row starts a document of its own.
All inputs are finite; a program needn't handle non-finite values.
Results may differ from the reference program's by a relative error of at most 0.018.
Values may be sent and summed in bfloat16 or wider, within the bound.
No kernel may reach another device: no remote copies, remote signals or barrier semaphores. Data moves between devices by JAX's collectives and lax.ppermute only.
A program may use at most 64 MiB of HBM per device.

```python
import jax
import jax.numpy as jnp
from jax import lax

D = 8192
QH = 64
KVH = 8
HEAD = 128
R = 512
PREFIX = 4096
LAYERS = 16


def draw_queries(key, part):
    key = jax.random.fold_in(key, 11)
    shape = (LAYERS, R, QH * HEAD)
    base = jnp.clip(jax.random.normal(key, shape, jnp.float32), -4.0, 4.0)
    return base.astype(jnp.bfloat16)


def draw_cache(key, part):
    key = jax.random.fold_in(key, 12)
    keys = jax.random.split(key, 3)
    means = jax.random.uniform(keys[1], (LAYERS, KVH, 1, HEAD), jnp.float32, -1.5, 1.5)
    cached_keys = jnp.clip(jax.random.normal(keys[0], (LAYERS, KVH * PREFIX, HEAD), jnp.float32), -4.0, 4.0)
    noise = jnp.clip(jax.random.normal(keys[2], (LAYERS, KVH, PREFIX, HEAD), jnp.float32), -3.0, 3.0)
    values = (means + noise).reshape(LAYERS, KVH * PREFIX, HEAD)
    return jnp.stack([cached_keys, values], axis=1).astype(jnp.bfloat16)


def draw_prefix_len(key, part):
    key = jax.random.fold_in(key, 13)
    keys = jax.random.split(key, 2)
    lengths = jax.random.randint(keys[0], (R,), PREFIX // 8, PREFIX + 1)
    chosen = jax.random.randint(keys[1], (), 0, R)
    return jnp.where(jnp.arange(R, dtype=jnp.int32) == chosen, PREFIX, lengths).astype(jnp.int32)


def draw_doc_start(key, part):
    key = jax.random.fold_in(key, 14)
    marks = jax.random.randint(key, (R,), 0, max(R // 8, 2)) == 0
    positions = jnp.arange(R, dtype=jnp.int32)
    marks = marks | (positions == 0) | (positions == R - 1)
    return lax.cummax(jnp.where(marks, positions, 0)).astype(jnp.int32)


def levels(key, dims, shards, smallest, high):
    loudness = 1.0
    for axis_at, shards_of in shards:
        draws = jax.random.uniform(jax.random.fold_in(jax.random.fold_in(key, 6), axis_at), (shards_of,), jnp.float32, smallest / len(shards), high / len(shards))
        loudness = loudness * jnp.repeat(jnp.exp(draws), dims[axis_at] // shards_of).reshape((-1,) + (1,) * (len(dims) - 1 - axis_at))
    return loudness


def gaussian(own_key, extent, deviation, bound, shards=(), held_as=jnp.bfloat16):
    drawn = deviation * jax.random.normal(own_key, extent, jnp.float32)
    if shards:
        drawn = drawn * levels(own_key, extent, shards, -0.22, 0.18)
    return jnp.clip(drawn, -bound, bound).astype(held_as)


def setup_inputs(seed: int = 0) -> dict:
    streams_of = jax.random.split(jax.random.key(seed), 8)
    hidden = gaussian(streams_of[0], (R, D), 1.0, 6.0, ((0, 16),))
    kv_weight = gaussian(streams_of[1], (LAYERS, 2 * KVH * HEAD, D), D ** -0.5, 0.0625, ((0, 16), (1, 32)))
    queries = draw_queries(jax.random.fold_in(streams_of[7], 71), 0)
    out_grads = gaussian(streams_of[3], (LAYERS, R, QH * HEAD), 64.0, 384.0, ((0, 16), (2, 32)))
    cache = draw_cache(jax.random.fold_in(streams_of[7], 71), 0)
    prefix_len = draw_prefix_len(jax.random.fold_in(streams_of[7], 71), 0)
    doc_start = draw_doc_start(jax.random.fold_in(streams_of[7], 71), 0)
    return dict(hidden=hidden, kv_weight=kv_weight, queries=queries, out_grads=out_grads, cache=cache, prefix_len=prefix_len, doc_start=doc_start)


def layer_grads(weight, queries, grads, cache, hidden, prefix_len, doc_start):
    group = QH // KVH
    softmax_scale = HEAD ** -0.5
    kv_new = jnp.dot(hidden, weight.T, preferred_element_type=jnp.float32).astype(jnp.bfloat16)
    kv_four = kv_new.astype(jnp.float32).reshape(R, KVH, 2, HEAD)
    fresh_keys = kv_four[:, :, 0]
    fresh_values = kv_four[:, :, 1]
    query_matrix = queries.astype(jnp.float32).reshape(R, KVH, group, HEAD)
    output_gradient = grads.astype(jnp.float32).reshape(R, KVH, group, HEAD)
    cached_keys = cache[0].astype(jnp.float32).reshape(KVH, PREFIX, HEAD)
    cached_values = cache[1].astype(jnp.float32).reshape(KVH, PREFIX, HEAD)
    scores_pre = jnp.einsum('rhgd,hjd->hgrj', query_matrix, cached_keys) * softmax_scale
    dots_pre = jnp.einsum('rhgd,hjd->hgrj', output_gradient, cached_values)
    fresh_scores = jnp.einsum('kica,eia->icke', query_matrix, fresh_keys) * softmax_scale
    fresh_logits = jnp.einsum('kica,eia->icke', output_gradient, fresh_values)
    seen = jnp.arange(PREFIX, dtype=jnp.int32)[None, :] < prefix_len[:, None]
    rows = jnp.arange(R, dtype=jnp.int32)
    mask_new = (rows[None, :] >= doc_start[:, None]) & (rows[None, :] <= rows[:, None])
    top = jnp.maximum(jnp.max(jnp.where(seen, scores_pre, -jnp.inf), axis=-1),
                      jnp.max(jnp.where(mask_new, fresh_scores, -jnp.inf), axis=-1))
    e_pre = jnp.exp(jnp.where(seen, scores_pre - top[..., None], -jnp.inf))
    e_new = jnp.exp(jnp.where(mask_new, fresh_scores - top[..., None], -jnp.inf))
    total = jnp.sum(e_pre, axis=-1) + jnp.sum(e_new, axis=-1)
    accum = jnp.sum(e_pre * dots_pre, axis=-1) + jnp.sum(e_new * fresh_logits, axis=-1)
    dsum = accum / total
    quotient = e_new / total[..., None]
    attention_weights = lax.optimization_barrier(quotient.astype(jnp.bfloat16)).astype(jnp.float32)
    score_gradient = (quotient * (fresh_logits - dsum[..., None])).astype(jnp.bfloat16)
    score_gradient = lax.optimization_barrier(score_gradient).astype(jnp.float32)
    value_gradient = jnp.einsum('tfeu,etfy->uty', attention_weights, output_gradient)
    key_gradient = jnp.einsum('tfeu,etfy->uty', score_gradient, query_matrix) * softmax_scale
    kv_grads = jnp.stack([key_gradient, value_gradient], axis=2).reshape(R, 2 * KVH * HEAD).astype(jnp.bfloat16)
    weight_grad = jnp.dot(kv_grads.T, hidden, preferred_element_type=jnp.float32)
    hidden_grad = jnp.dot(kv_grads, weight, preferred_element_type=jnp.float32)
    return weight_grad, hidden_grad


def reference(hidden, kv_weight, queries, out_grads, cache, prefix_len, doc_start):
    def one_layer(items):
        return layer_grads(items[0], items[1], items[2], items[3], hidden, prefix_len, doc_start)

    weight_grads, hidden_terms = lax.map(one_layer, (kv_weight, queries, out_grads, cache))
    hidden_grads = jnp.sum(hidden_terms, axis=0)
    return hidden_grads, weight_grads
```

```python
import functools

import jax
import jax.numpy as jnp
from jax import lax
from jax.experimental import pallas as pl
from jax.experimental.pallas import tpu as pltpu
from jax.sharding import Mesh, PartitionSpec as P

HEAD = 128
R = 512
POSITIONS = 1024
TOKENS = 128
SCALE = HEAD**-0.5
LOG2E = 1.4426950408889634
LOW = -1e30
PLANE = ("yh", "yl", "core")
QUAD = ("yl", "core")
NT = (((1,), (1,)), ((), ()))


def swapped(value, axes, moved):
    count = 1
    for axis in axes:
        count *= lax.axis_size(axis)
    pairs = [(source, source ^ moved) for source in range(count)]
    return lax.ppermute(value, axes, pairs)


def softmax_parts(scores, dots):
    top = jnp.max(scores, axis=0, keepdims=True)
    weights = jnp.exp2((scores - top) * (SCALE * LOG2E))
    total = jnp.sum(weights, axis=0, keepdims=True)
    accum = jnp.sum(weights * dots, axis=0, keepdims=True)
    return top, total, accum


def merged(first, second):
    top = jnp.maximum(first[0], second[0])
    fade_first = jnp.exp2((first[0] - top) * (SCALE * LOG2E))
    fade_second = jnp.exp2((second[0] - top) * (SCALE * LOG2E))
    return (
        top,
        first[1] * fade_first + second[1] * fade_second,
        first[2] * fade_first + second[2] * fade_second,
    )


def prefix_kernel(place, q0, o0, p1, p2, p3, cache, prefix_len, stats):
    rank = place[0]
    lengths = prefix_len[...]
    chunk = 512
    for other, (q, o) in enumerate(
        ((q0, o0), (p1.at[0], p1.at[1]), (p2.at[0], p2.at[1]), (p3.at[0], p3.at[1]))
    ):
        for head in range(2):
            columns = pl.ds(head * HEAD, HEAD)
            queries = q[:, columns]
            grads = o[:, columns]

            parts = None
            for start in range(0, POSITIONS, chunk):
                rows = pl.ds(start, chunk)
                scores = lax.dot_general(
                    cache[0, rows, :], queries, NT, preferred_element_type=jnp.float32
                )
                dots = lax.dot_general(
                    cache[1, rows, :], grads, NT, preferred_element_type=jnp.float32
                )
                ids = lax.broadcasted_iota(jnp.int32, (chunk, R), 0)
                limit = lengths - (rank * POSITIONS + start)
                piece = softmax_parts(jnp.where(ids < limit, scores, LOW), dots)
                parts = piece if parts is None else merged(parts, piece)
            slot = (rank ^ other) * 2 + head
            for kind in range(3):
                stats[kind, pl.ds(slot, 1), :] = parts[kind]


def new_scores(rank, ids_ref, doc_start, keys, values, queries, grads):
    scores = lax.dot_general(keys, queries, NT, preferred_element_type=jnp.float32)
    dots = lax.dot_general(values, grads, NT, preferred_element_type=jnp.float32)
    place = lax.broadcasted_iota(jnp.int32, (TOKENS, R), 0)
    token = (place // 32) * 128 + rank * 32 + place % 32
    row = lax.broadcasted_iota(jnp.int32, (TOKENS, R), 1)
    mask = (token >= doc_start) & (token <= row)
    return jnp.where(mask, scores, LOW), dots


def new_stats_kernel(place, partial, q0, o0, p1, p2, p3, doc_start, before, stats, kv):
    rank = place[0]
    total_kv = partial[0].astype(jnp.float32)
    for source in range(1, 8):
        total_kv = total_kv + partial[source].astype(jnp.float32)
    kv[...] = total_kv.astype(jnp.bfloat16)
    starts = doc_start[...]
    for other, (q, o) in enumerate(
        ((q0, o0), (p1.at[0], p1.at[1]), (p2.at[0], p2.at[1]), (p3.at[0], p3.at[1]))
    ):
        for head in range(2):
            columns = pl.ds(head * HEAD, HEAD)
            scores, dots = new_scores(
                rank, None, starts, kv[:, :HEAD], kv[:, HEAD:], q[:, columns], o[:, columns]
            )
            slot = pl.ds((rank ^ other) * 2 + head, 1)
            parts = merged(
                softmax_parts(scores, dots), tuple(before[kind, slot, :] for kind in range(3))
            )
            for kind in range(3):
                stats[kind, slot, :] = parts[kind]


def new_grads_kernel(place, kv, q0, o0, p1, p2, p3, doc_start, every, out, whole, key_sum, value_sum):
    rank = place[0]
    top = jnp.maximum(
        jnp.maximum(every[0, 0], every[1, 0]), jnp.maximum(every[2, 0], every[3, 0])
    )
    total = jnp.zeros_like(top)
    accum = jnp.zeros_like(top)
    for member in range(4):
        fade = jnp.exp2((every[member, 0] - top) * (SCALE * LOG2E))
        total = total + every[member, 1] * fade
        accum = accum + every[member, 2] * fade
    whole[0] = top
    whole[1] = 1.0 / total
    whole[2] = accum / total
    starts = doc_start[...]
    for other, (q, o) in enumerate(
        ((q0, o0), (p1.at[0], p1.at[1]), (p2.at[0], p2.at[1]), (p3.at[0], p3.at[1]))
    ):
        for head in range(2):
            columns = pl.ds(head * HEAD, HEAD)
            queries = q[:, columns]
            grads = o[:, columns]
            scores, dots = new_scores(
                rank, None, starts, kv[:, :HEAD], kv[:, HEAD:], queries, grads
            )
            slot = pl.ds((rank ^ other) * 2 + head, 1)
            quotient = jnp.exp2((scores - whole[0, slot, :]) * (SCALE * LOG2E)) * whole[1, slot, :]
            probs = quotient.astype(jnp.bfloat16)
            dscores = (quotient * (dots - whole[2, slot, :])).astype(jnp.bfloat16)
            key_part = jnp.dot(dscores, queries, preferred_element_type=jnp.float32)
            value_part = jnp.dot(probs, grads, preferred_element_type=jnp.float32)
            if other == 0 and head == 0:
                key_sum[...] = key_part
                value_sum[...] = value_part
            else:
                key_sum[...] += key_part
                value_sum[...] += value_part
    out[:, :HEAD] = (key_sum[...] * SCALE).astype(jnp.bfloat16)
    out[:, HEAD:] = value_sum[...].astype(jnp.bfloat16)


def called(kernel, out_shape, operands, flops, moved, scratch=()):
    vmem = pl.BlockSpec(memory_space=pltpu.VMEM)
    return pl.pallas_call(
        kernel,
        out_shape=out_shape,
        in_specs=[pl.BlockSpec(memory_space=pltpu.SMEM)] + [vmem] * (len(operands) - 1),
        out_specs=jax.tree.map(lambda leaf: vmem, out_shape),
        scratch_shapes=list(scratch),
        compiler_params=pltpu.CompilerParams(vmem_limit_bytes=32 * 1024 * 1024),
        cost_estimate=pl.CostEstimate(
            flops=flops, bytes_accessed=moved, transcendentals=flops // 512
        ),
    )(*operands)


def shards(hidden, kv_weight, queries, out_grads, cache, prefix_len, doc_start):
    plane_rank = lax.axis_index(PLANE)
    rank = lax.axis_index(QUAD)
    place = jnp.reshape(rank, (1,)).astype(jnp.int32)
    width = hidden.shape[1] // 8

    q0 = queries[0]
    o0 = out_grads[0]
    pair = jnp.stack([q0, o0])
    p2 = swapped(pair, QUAD, 2)
    p1 = swapped(pair, QUAD, 1)
    p3 = swapped(p2, QUAD, 1)

    turned = kv_weight[0].reshape(64, 4, 8, width // 4).transpose(2, 0, 1, 3).reshape(8, 64, width)
    turned = lax.all_to_all(turned, PLANE, 0, 0, tiled=True)

    own = lax.dynamic_index_in_dim(hidden.reshape(32, 4, 8, width // 4), plane_rank, 2, False)
    own = lax.all_gather(own.reshape(32, width), "zh", axis=0, tiled=True)
    states = lax.all_to_all(jnp.broadcast_to(own, (4, *own.shape)), "x", 0, 0, tiled=True)
    states = states.reshape(R, width)

    heads = turned.reshape(2, 256, width)
    partial = [
        lax.dot_general(states, heads[j], NT, preferred_element_type=jnp.float32).astype(
            jnp.bfloat16
        )
        for j in range(2)
    ]
    partial = jnp.stack(partial).reshape(8, TOKENS, 256)
    partial = lax.all_to_all(partial, PLANE, 0, 0, tiled=True)

    lengths = prefix_len.reshape(1, R)
    starts = doc_start.reshape(1, R)
    stats_shape = jax.ShapeDtypeStruct((3, 8, R), jnp.float32)
    before = called(
        prefix_kernel,
        stats_shape,
        (place, q0, o0, p1, p2, p3, cache[0], lengths),
        2 * 2 * 8 * R * POSITIONS * HEAD * 4,
        3 << 20,
    )
    stats, kv = called(
        new_stats_kernel,
        (stats_shape, jax.ShapeDtypeStruct((TOKENS, 256), jnp.bfloat16)),
        (place, partial, q0, o0, p1, p2, p3, starts, before),
        2 * 2 * 8 * R * TOKENS * HEAD * 4,
        3 << 20,
    )
    every = lax.all_gather(stats, QUAD, axis=0)
    grads = called(
        new_grads_kernel,
        jax.ShapeDtypeStruct((TOKENS, 256), jnp.bfloat16),
        (place, kv, q0, o0, p1, p2, p3, starts, every),
        4 * 2 * 8 * R * TOKENS * HEAD * 4,
        3 << 20,
        (
            pltpu.VMEM((3, 8, R), jnp.float32),
            pltpu.VMEM((TOKENS, HEAD), jnp.float32),
            pltpu.VMEM((TOKENS, HEAD), jnp.float32),
        ),
    )
    kv_grads = lax.all_gather(grads, PLANE, axis=0, tiled=True).reshape(2, R, 256)

    hidden_part = jnp.dot(kv_grads[0], heads[0], preferred_element_type=jnp.float32)
    hidden_part = hidden_part + jnp.dot(kv_grads[1], heads[1], preferred_element_type=jnp.float32)
    hidden_part = hidden_part.astype(jnp.bfloat16).reshape(4, 128, width)
    over_x = lax.all_to_all(hidden_part, "x", 0, 0, tiled=True)
    over_x = jnp.sum(over_x.astype(jnp.float32), axis=0).astype(jnp.bfloat16)
    over_x = over_x.reshape(4, 32, 4, width // 4).transpose(0, 2, 1, 3).reshape(16, 32, width // 4)
    over_z = lax.all_to_all(over_x, ("zh", "zl"), 0, 0, tiled=True)
    hidden_grads = jnp.sum(over_z.astype(jnp.float32), axis=0)

    weight_part = lax.dot_general(
        kv_grads, states, (((1,), (0,)), ((), ())), preferred_element_type=jnp.float32
    )
    weight_part = weight_part.astype(jnp.bfloat16).reshape(8, 64, width)
    weight_part = lax.all_to_all(weight_part, PLANE, 0, 0, tiled=True)
    weight_grads = (
        weight_part.reshape(8, 64, 4, width // 4).transpose(1, 2, 0, 3).reshape(1, 64, 8 * width)
    )
    return hidden_grads, weight_grads.astype(jnp.float32)


def solution(mesh):
    axes = ("zh", "x", "zl", "yh", "yl", "core")
    split = Mesh(mesh.devices.reshape(4, 4, 4, 2, 2, 2), axes)
    pipe = ("zh", "x")
    tensor = ("zl", "yh", "yl", "core")
    return jax.shard_map(
        shards,
        mesh=split,
        in_specs=(
            P(pipe, None),
            P(pipe, tensor, None),
            P(pipe, None, tensor),
            P(pipe, None, tensor),
            P(pipe, None, tensor, None),
            P(),
            P(),
        ),
        out_specs=(P(pipe, tensor), P(pipe, tensor, None)),
        check_vma=False,
    )
```

```python
import functools

import jax
import jax.numpy as jnp
from jax import lax
from jax.experimental import pallas as pl
from jax.experimental.pallas import tpu as pltpu
from jax.sharding import Mesh, PartitionSpec as P

HEAD = 128
R = 512
POSITIONS = 1024
TOKENS = 128
SCALE = HEAD**-0.5
LOG2E = 1.4426950408889634
LOW = -1e30
PLANE = ("yh", "yl", "core")
QUAD = ("yl", "core")
NT = (((1,), (1,)), ((), ()))


def swapped(value, axes, moved):
    count = 1
    for axis in axes:
        count *= lax.axis_size(axis)
    pairs = [(source, source ^ moved) for source in range(count)]
    return lax.ppermute(value, axes, pairs)


def softmax_parts(scores, dots):
    top = jnp.max(scores, axis=0, keepdims=True)
    weights = jnp.exp2((scores - top) * (SCALE * LOG2E))
    total = jnp.sum(weights, axis=0, keepdims=True)
    accum = jnp.sum(weights * dots, axis=0, keepdims=True)
    return top, total, accum


def merged(first, second):
    top = jnp.maximum(first[0], second[0])
    fade_first = jnp.exp2((first[0] - top) * (SCALE * LOG2E))
    fade_second = jnp.exp2((second[0] - top) * (SCALE * LOG2E))
    return (
        top,
        first[1] * fade_first + second[1] * fade_second,
        first[2] * fade_first + second[2] * fade_second,
    )


def fetch(moves, sems):
    copies = [
        pltpu.make_async_copy(source, target, sems.at[index])
        for index, (source, target) in enumerate(moves)
    ]
    for copy in copies:
        copy.start()
    return copies


def fetch_pairs(sources, pairs, sems):
    moves = []
    for index, source in enumerate(sources):
        if isinstance(source, tuple):
            moves += [(part, pairs.at[index, kind]) for kind, part in enumerate(source)]
        else:
            moves += [(source.at[kind], pairs.at[index, kind]) for kind in range(2)]
    return fetch(moves, sems)


def prefix_stats(rank, lengths, sources, cache, stats, blocks, pairs, sems):
    chunk = 512
    base = pltpu.make_async_copy(cache, blocks, sems.at[4])
    base.start()
    copies = fetch_pairs(sources, pairs, sems)
    base.wait()
    for other in range(2):
        copies[2 * other].wait()
        copies[2 * other + 1].wait()
        for head in range(2):
            columns = pl.ds(head * HEAD, HEAD)
            queries = pairs[other, 0, :, columns]
            grads = pairs[other, 1, :, columns]
            parts = None
            for start in range(0, POSITIONS, chunk):
                rows = pl.ds(start, chunk)
                scores = lax.dot_general(
                    blocks[0, rows, :], queries, NT, preferred_element_type=jnp.float32
                )
                dots = lax.dot_general(
                    blocks[1, rows, :], grads, NT, preferred_element_type=jnp.float32
                )
                ids = lax.broadcasted_iota(jnp.int32, (chunk, R), 0)
                limit = lengths - (rank * POSITIONS + start)
                piece = softmax_parts(jnp.where(ids < limit, scores, LOW), dots)
                parts = piece if parts is None else merged(parts, piece)
            for kind in range(3):
                stats[kind, pl.ds(other * 2 + head, 1), :] = parts[kind]


def near_prefix_kernel(place, prefix_len, cache, q0, o0, p1, stats, *scratch):
    prefix_stats(place[0], prefix_len[...], ((q0, o0), p1), cache, stats, *scratch)


def far_prefix_kernel(place, prefix_len, cache, p2, p3, stats, *scratch):
    prefix_stats(place[0], prefix_len[...], (p2, p3), cache, stats, *scratch)


def new_scores(rank, doc_start, keys, values, queries, grads):
    scores = lax.dot_general(keys, queries, NT, preferred_element_type=jnp.float32)
    dots = lax.dot_general(values, grads, NT, preferred_element_type=jnp.float32)
    place = lax.broadcasted_iota(jnp.int32, (TOKENS, R), 0)
    token = (place // 32) * 128 + rank * 32 + place % 32
    row = lax.broadcasted_iota(jnp.int32, (TOKENS, R), 1)
    mask = (token >= doc_start) & (token <= row)
    return jnp.where(mask, scores, LOW), dots


def new_stats_kernel(
    place, doc_start, first, second, partial, q0, o0, p1, p2, p3, stats, kv, pairs, blocks, sems
):
    rank = place[0]
    base = pltpu.make_async_copy(partial, blocks, sems.at[8])
    base.start()
    copies = fetch_pairs(((q0, o0), p1, p2, p3), pairs, sems)
    base.wait()
    total_kv = blocks[0].astype(jnp.float32)
    for source in range(1, 8):
        total_kv = total_kv + blocks[source].astype(jnp.float32)
    kv[...] = total_kv.astype(jnp.bfloat16)
    starts = doc_start[...]
    for other in range(4):
        copies[2 * other].wait()
        copies[2 * other + 1].wait()
        before = first if other < 2 else second
        for head in range(2):
            columns = pl.ds(head * HEAD, HEAD)
            scores, dots = new_scores(
                rank,
                starts,
                kv[:, :HEAD],
                kv[:, HEAD:],
                pairs[other, 0, :, columns],
                pairs[other, 1, :, columns],
            )
            held = pl.ds(other % 2 * 2 + head, 1)
            parts = merged(
                softmax_parts(scores, dots), tuple(before[kind, held, :] for kind in range(3))
            )
            slot = pl.ds((rank ^ other) * 2 + head, 1)
            for kind in range(3):
                stats[kind, slot, :] = parts[kind]


def new_grads_kernel(
    place, kv, pairs, doc_start, every, out, whole, key_sum, value_sum
):
    rank = place[0]
    top = jnp.maximum(
        jnp.maximum(every[0, 0], every[1, 0]), jnp.maximum(every[2, 0], every[3, 0])
    )
    total = jnp.zeros_like(top)
    accum = jnp.zeros_like(top)
    for member in range(4):
        fade = jnp.exp2((every[member, 0] - top) * (SCALE * LOG2E))
        total = total + every[member, 1] * fade
        accum = accum + every[member, 2] * fade
    whole[0] = top
    whole[1] = 1.0 / total
    whole[2] = accum / total
    starts = doc_start[...]
    for other in range(4):
        for head in range(2):
            columns = pl.ds(head * HEAD, HEAD)
            queries = pairs[other, 0, :, columns]
            grads = pairs[other, 1, :, columns]
            scores, dots = new_scores(
                rank, starts, kv[:, :HEAD], kv[:, HEAD:], queries, grads
            )
            slot = pl.ds((rank ^ other) * 2 + head, 1)
            quotient = jnp.exp2((scores - whole[0, slot, :]) * (SCALE * LOG2E)) * whole[1, slot, :]
            probs = quotient.astype(jnp.bfloat16)
            dscores = (quotient * (dots - whole[2, slot, :])).astype(jnp.bfloat16)
            key_part = jnp.dot(dscores, queries, preferred_element_type=jnp.float32)
            value_part = jnp.dot(probs, grads, preferred_element_type=jnp.float32)
            if other == 0 and head == 0:
                key_sum[...] = key_part
                value_sum[...] = value_part
            else:
                key_sum[...] += key_part
                value_sum[...] += value_part
    out[:, :HEAD] = (key_sum[...] * SCALE).astype(jnp.bfloat16)
    out[:, HEAD:] = value_sum[...].astype(jnp.bfloat16)


def arrange_kernel(
    place, weight, hidden, queries, grads, turned, own, pair, blocks, both, arrived, left
):
    width = own.shape[1] // 4
    columns = [pl.ds(part * width, width) for part in range(4)]
    moves = [
        (weight.at[:, pl.ds((part * 8 + member) * width, width)], blocks.at[member, :, columns[part]])
        for member in range(8)
        for part in range(4)
    ]
    for part in range(4):
        start = pl.multiple_of((part * 8 + place[0]) * width, width)
        moves.append((hidden.at[:, pl.ds(start, width)], own.at[:, columns[part]]))
    moves += [(queries, both.at[0]), (grads, both.at[1])]
    copies = fetch(moves, arrived)
    sent = [
        pltpu.make_async_copy(blocks.at[member], turned.at[member], left.at[member])
        for member in range(8)
    ]
    sent += [pltpu.make_async_copy(both.at[kind], pair.at[kind], left.at[8 + kind]) for kind in range(2)]
    for member in range(8):
        for copy in copies[4 * member : 4 * member + 4]:
            copy.wait()
        sent[member].start()
    for kind in range(2):
        copies[36 + kind].wait()
        sent[8 + kind].start()
    for copy in copies[32:36] + sent:
        copy.wait()


def repeat_kernel(block, out):
    for index in range(out.shape[0]):
        out[index] = block[...]


def project_kernel(states, heads, out):
    for head in range(2):
        product = lax.dot_general(
            states[...], heads[head], NT, preferred_element_type=jnp.float32
        ).astype(jnp.bfloat16)
        for quarter in range(4):
            out[head * 4 + quarter] = product[quarter * TOKENS : (quarter + 1) * TOKENS]


def hidden_kernel(kv_grads, heads, out, parts, sems):
    copies = []
    for quarter in range(4):
        rows = pl.ds(quarter * TOKENS, TOKENS)
        parts[quarter] = (
            jnp.dot(kv_grads[0, rows, :], heads[0], preferred_element_type=jnp.float32)
            + jnp.dot(kv_grads[1, rows, :], heads[1], preferred_element_type=jnp.float32)
        ).astype(jnp.bfloat16)
        copy = pltpu.make_async_copy(parts.at[quarter], out.at[quarter], sems.at[quarter])
        copy.start()
        copies.append(copy)
    for copy in copies:
        copy.wait()


def weight_kernel(place, kv_grads, states, mine, one, three, rows):
    for head in range(2):
        rows[head * 256 : (head + 1) * 256, :] = lax.dot_general(
            kv_grads[head],
            states[...],
            (((0,), (0,)), ((), ())),
            preferred_element_type=jnp.float32,
        ).astype(jnp.bfloat16)

    def block(chip, core, start, count):
        first = ((place[0] // 2) ^ chip) * 128 + core * 64 + start
        return rows[pl.ds(pl.multiple_of(first, 32), count), :]

    for core in range(2):
        mine[core] = block(0, core, 0, 64)
        one[core, :64] = block(1, core, 0, 64)
        one[core, 64:] = block(2, core, 0, 32)
        three[core, :64] = block(3, core, 0, 64)
        three[core, 64:] = block(2, core, 32, 32)


def cores_kernel(place, mine, one, three, upper, lower, kept, passed):
    for out, core in ((kept, place[0] % 2), (passed, 1 - place[0] % 2)):
        out[0] = mine[core]
        out[1] = one[core, :64]
        out[2, :32] = upper[core]
        out[2, 32:] = lower[core]
        out[3] = three[core, :64]


def place_kernel(place, kept, taken, out):
    width = kept.shape[2] // 4
    for chip in range(4):
        for core, blocks in enumerate((kept, taken)):
            for part in range(4):
                member = place[0] ^ (chip * 2 + core)
                start = pl.multiple_of((part * 8 + member) * width, width)
                out[0, :, pl.ds(start, width)] = blocks[
                    chip, :, part * width : (part + 1) * width
                ].astype(jnp.float32)


def reduce_x_kernel(blocks, out):
    width = blocks.shape[2] // 4
    for high in range(4):
        rows = pl.ds(high * 32, 32)
        total = blocks[0, rows, :].astype(jnp.float32)
        for source in range(1, 4):
            total = total + blocks[source, rows, :].astype(jnp.float32)
        total = total.astype(jnp.bfloat16)
        for low in range(4):
            out[high * 4 + low] = total[:, low * width : (low + 1) * width]


def called(
    kernel, out_shape, operands, flops, moved, scratch=(), places=(), outs=None, limit=12, grid=()
):
    vmem = pl.BlockSpec(memory_space=pltpu.VMEM)
    return pl.pallas_call(
        kernel,
        grid=grid,
        out_shape=out_shape,
        in_specs=list(places) + [vmem] * (len(operands) - len(places)),
        out_specs=jax.tree.map(lambda leaf: vmem, out_shape) if outs is None else outs,
        scratch_shapes=list(scratch),
        compiler_params=pltpu.CompilerParams(vmem_limit_bytes=limit * 1024 * 1024),
        cost_estimate=pl.CostEstimate(
            flops=flops, bytes_accessed=moved, transcendentals=flops // 512
        ),
    )(*operands)


def shaped(dtype, *shape):
    return jax.ShapeDtypeStruct(shape, dtype)


def shards(hidden, kv_weight, queries, out_grads, cache, prefix_len, doc_start):
    plane_rank = lax.axis_index(PLANE)
    rank = lax.axis_index(QUAD)
    member = jnp.reshape(plane_rank, (1,)).astype(jnp.int32)
    place = jnp.reshape(rank, (1,)).astype(jnp.int32)
    width = hidden.shape[1] // 8
    bf16 = jnp.bfloat16
    f32 = jnp.float32
    smem = pl.BlockSpec(memory_space=pltpu.SMEM)
    vmem = pl.BlockSpec(memory_space=pltpu.VMEM)
    anywhere = pl.BlockSpec(memory_space=pl.ANY)
    hbm = pl.BlockSpec(memory_space=pltpu.HBM)
    dma = pltpu.SemaphoreType.DMA

    def far(value):
        return pltpu.with_memory_space_constraint(value, pltpu.HBM)

    q0 = queries[0]
    o0 = out_grads[0]
    turned, own, pair = called(
        arrange_kernel,
        (shaped(bf16, 8, 64, width), shaped(bf16, 32, width), shaped(bf16, 2, R, 256)),
        (member, far(kv_weight[0]), far(hidden), far(q0), far(o0)),
        0,
        4 << 20,
        (
            pltpu.VMEM((8, 64, width), bf16),
            pltpu.VMEM((2, R, 256), bf16),
            dma((38,)),
            dma((10,)),
        ),
        (smem, hbm, hbm, hbm, hbm),
        (anywhere, vmem, anywhere),
    )

    turned = lax.all_to_all(turned, PLANE, 0, 0, tiled=True)

    own = lax.all_gather(own, "zh", axis=0, tiled=True)
    own, turned, pair = lax.optimization_barrier((own, turned, pair))
    states = called(repeat_kernel, shaped(bf16, 4, 128, width), (own,), 0, 1 << 20)
    states = lax.all_to_all(states, "x", 0, 0, tiled=True)

    p2 = swapped(pair, QUAD, 2)
    p1 = swapped(pair, QUAD, 1)
    states = states.reshape(R, width)
    heads = turned.reshape(2, 256, width)
    partial = called(
        project_kernel,
        shaped(bf16, 8, TOKENS, 256),
        (states, heads),
        2 * R * 512 * width,
        3 << 20,
    )
    p2, partial = lax.optimization_barrier((p2, partial))
    p3 = swapped(p2, QUAD, 1)
    partial = lax.all_to_all(partial, PLANE, 0, 0, tiled=True)

    lengths = prefix_len.reshape(1, R)
    starts = doc_start.reshape(1, R)

    def prefix(kernel, *operands):
        return called(
            kernel,
            shaped(f32, 3, 4, R),
            (place, lengths, *(far(operand) for operand in (cache[0], *operands))),
            2 * 2 * 4 * R * POSITIONS * HEAD * 4,
            2 << 20,
            (pltpu.VMEM((2, POSITIONS, HEAD), bf16), pltpu.VMEM((2, 2, R, 256), bf16), dma((5,))),
            (smem, vmem) + (hbm,) * (1 + len(operands)),
            limit=20,
        )

    first = prefix(near_prefix_kernel, q0, o0, p1)
    second = prefix(far_prefix_kernel, p2, p3)
    stats, kv, pairs = called(
        new_stats_kernel,
        (shaped(f32, 3, 8, R), shaped(bf16, TOKENS, 256), shaped(bf16, 4, 2, R, 256)),
        (place, starts, first, second, partial, *(far(operand) for operand in (q0, o0, p1, p2, p3))),
        2 * 2 * 8 * R * TOKENS * HEAD * 4,
        3 << 20,
        (pltpu.VMEM((8, TOKENS, 256), bf16), dma((9,))),
        (smem, vmem, vmem, vmem, anywhere) + (hbm,) * 5,
    )
    every = lax.all_gather(stats, QUAD, axis=0)
    grads = called(
        new_grads_kernel,
        shaped(bf16, TOKENS, 256),
        (place, kv, pairs, starts, every),
        4 * 2 * 8 * R * TOKENS * HEAD * 4,
        3 << 20,
        (
            pltpu.VMEM((3, 8, R), f32),
            pltpu.VMEM((TOKENS, HEAD), f32),
            pltpu.VMEM((TOKENS, HEAD), f32),
        ),
        (smem,),
    )
    kv_grads = lax.all_gather(grads, PLANE, axis=0, tiled=True).reshape(2, R, 256)

    hidden_part = called(
        hidden_kernel,
        shaped(bf16, 4, TOKENS, width),
        (kv_grads, heads),
        2 * R * 512 * width,
        3 << 20,
        (pltpu.VMEM((4, TOKENS, width), bf16), dma((4,))),
        outs=anywhere,
    )
    hidden_part, kv_grads = lax.optimization_barrier((hidden_part, kv_grads))
    over_x = lax.all_to_all(hidden_part, "x", 0, 0, tiled=True)
    over_x = called(reduce_x_kernel, shaped(bf16, 16, 32, width // 4), (over_x,), 0, 1 << 20)

    mine, one, three = called(
        weight_kernel,
        (shaped(bf16, 2, 64, width),) + (shaped(bf16, 2, 96, width),) * 2,
        (member, kv_grads, states),
        2 * R * 512 * width,
        3 << 20,
        (pltpu.VMEM((512, width), bf16),),
        (smem,),
    )
    one = swapped(one, PLANE, 2)
    three = swapped(three, PLANE, 6)
    over_x, one, three = lax.optimization_barrier((over_x, one, three))
    over_z = lax.all_to_all(over_x, ("zh", "zl"), 0, 0, tiled=True)
    hidden_grads = jnp.sum(over_z.astype(f32), axis=0)

    upper = swapped(one[:, 64:], PLANE, 6)
    lower = swapped(three[:, 64:], PLANE, 2)
    kept, passed = called(
        cores_kernel,
        (shaped(bf16, 4, 64, width),) * 2,
        (member, mine, one, three, upper, lower),
        0,
        1 << 20,
        (),
        (smem,),
    )
    taken = swapped(passed, PLANE, 1)
    weight_grads = called(
        place_kernel,
        shaped(f32, 1, 64, 8 * width),
        (member, kept, taken),
        0,
        3 << 20,
        (),
        (smem,),
    )
    return hidden_grads, weight_grads


def solution(mesh):
    axes = ("zh", "x", "zl", "yh", "yl", "core")
    split = Mesh(mesh.devices.reshape(4, 4, 4, 2, 2, 2), axes)
    pipe = ("zh", "x")
    tensor = ("zl", "yh", "yl", "core")
    return jax.shard_map(
        shards,
        mesh=split,
        in_specs=(
            P(pipe, None),
            P(pipe, tensor, None),
            P(pipe, None, tensor),
            P(pipe, None, tensor),
            P(pipe, None, tensor, None),
            P(),
            P(),
        ),
        out_specs=(P(pipe, tensor), P(pipe, tensor, None)),
        check_vma=False,
    )
```

```python
import functools

import jax
import jax.numpy as jnp
from jax import lax
from jax.experimental import pallas as pl
from jax.experimental.pallas import tpu as pltpu
from jax.sharding import Mesh, PartitionSpec as P

HEAD = 128
R = 512
POSITIONS = 1024
TOKENS = 128
SCALE = HEAD**-0.5
LOG2E = 1.4426950408889634
LOW = -1e30
PLANE = ("yh", "yl", "core")
QUAD = ("yl", "core")
NT = (((1,), (1,)), ((), ()))


def swapped(value, axes, moved):
    count = 1
    for axis in axes:
        count *= lax.axis_size(axis)
    pairs = [(source, source ^ moved) for source in range(count)]
    return lax.ppermute(value, axes, pairs)


def softmax_parts(scores, dots):
    top = jnp.max(scores, axis=0, keepdims=True)
    weights = jnp.exp2((scores - top) * (SCALE * LOG2E))
    total = jnp.sum(weights, axis=0, keepdims=True)
    accum = jnp.sum(weights * dots, axis=0, keepdims=True)
    return top, total, accum


def merged(first, second):
    top = jnp.maximum(first[0], second[0])
    fade_first = jnp.exp2((first[0] - top) * (SCALE * LOG2E))
    fade_second = jnp.exp2((second[0] - top) * (SCALE * LOG2E))
    return (
        top,
        first[1] * fade_first + second[1] * fade_second,
        first[2] * fade_first + second[2] * fade_second,
    )


def fetch(moves, sems):
    copies = [
        pltpu.make_async_copy(source, target, sems.at[index])
        for index, (source, target) in enumerate(moves)
    ]
    for copy in copies:
        copy.start()
    return copies


def prefix_kernel(place, prefix_len, cache, beside, q0, o0, p2, stats):
    rank = place[0]
    lengths = prefix_len[...]
    chunk = 512
    for other, (q, o) in enumerate(((q0, o0), (p2.at[0], p2.at[1]))):
        for head in range(2):
            columns = pl.ds(head * HEAD, HEAD)
            queries = q[:, columns]
            grads = o[:, columns]
            parts = None
            for core, blocks in enumerate((cache, beside)):
                for start in range(0, POSITIONS, chunk):
                    rows = pl.ds(start, chunk)
                    scores = lax.dot_general(
                        blocks[0, rows, :], queries, NT, preferred_element_type=jnp.float32
                    )
                    dots = lax.dot_general(
                        blocks[1, rows, :], grads, NT, preferred_element_type=jnp.float32
                    )
                    ids = lax.broadcasted_iota(jnp.int32, (chunk, R), 0)
                    limit = lengths - ((rank ^ core) * POSITIONS + start)
                    piece = softmax_parts(jnp.where(ids < limit, scores, LOW), dots)
                    parts = piece if parts is None else merged(parts, piece)
            for kind in range(3):
                stats[kind, pl.ds(other * 2 + head, 1), :] = parts[kind]


def new_scores(rank, doc_start, keys, values, queries, grads):
    scores = lax.dot_general(keys, queries, NT, preferred_element_type=jnp.float32)
    dots = lax.dot_general(values, grads, NT, preferred_element_type=jnp.float32)
    place = lax.broadcasted_iota(jnp.int32, (TOKENS, R), 0)
    token = (place // 32) * 128 + rank * 32 + place % 32
    row = lax.broadcasted_iota(jnp.int32, (TOKENS, R), 1)
    mask = (token >= doc_start) & (token <= row)
    return jnp.where(mask, scores, LOW), dots


def new_stats_kernel(
    place, doc_start, before, partial, q0, o0, p1, p2, p3, stats, kv, pairs, sems
):
    rank = place[0]
    sources = ((q0, o0), (p1.at[0], p1.at[1]), (p2.at[0], p2.at[1]), (p3.at[0], p3.at[1]))
    copies = fetch(
        [
            (part, pairs.at[other, kind])
            for other, source in enumerate(sources)
            for kind, part in enumerate(source)
        ],
        sems,
    )
    total_kv = partial[0].astype(jnp.float32)
    for source in range(1, 8):
        total_kv = total_kv + partial[source].astype(jnp.float32)
    kv[...] = total_kv.astype(jnp.bfloat16)
    starts = doc_start[...]
    for other in range(4):
        copies[2 * other].wait()
        copies[2 * other + 1].wait()
        for head in range(2):
            columns = pl.ds(head * HEAD, HEAD)
            scores, dots = new_scores(
                rank,
                starts,
                kv[:, :HEAD],
                kv[:, HEAD:],
                pairs[other, 0, :, columns],
                pairs[other, 1, :, columns],
            )
            parts = softmax_parts(scores, dots)
            if other % 2 == 0:
                held = pl.ds(other + head, 1)
                parts = merged(parts, tuple(before[kind, held, :] for kind in range(3)))
            slot = pl.ds((rank ^ other) * 2 + head, 1)
            for kind in range(3):
                stats[kind, slot, :] = parts[kind]


def new_grads_kernel(
    place, kv, pairs, doc_start, every, out, whole, key_sum, value_sum
):
    rank = place[0]
    top = jnp.maximum(
        jnp.maximum(every[0, 0], every[1, 0]), jnp.maximum(every[2, 0], every[3, 0])
    )
    total = jnp.zeros_like(top)
    accum = jnp.zeros_like(top)
    for member in range(4):
        fade = jnp.exp2((every[member, 0] - top) * (SCALE * LOG2E))
        total = total + every[member, 1] * fade
        accum = accum + every[member, 2] * fade
    whole[0] = top
    whole[1] = 1.0 / total
    whole[2] = accum / total
    starts = doc_start[...]
    for other in range(4):
        for head in range(2):
            columns = pl.ds(head * HEAD, HEAD)
            queries = pairs[other, 0, :, columns]
            grads = pairs[other, 1, :, columns]
            scores, dots = new_scores(
                rank, starts, kv[:, :HEAD], kv[:, HEAD:], queries, grads
            )
            slot = pl.ds((rank ^ other) * 2 + head, 1)
            quotient = jnp.exp2((scores - whole[0, slot, :]) * (SCALE * LOG2E)) * whole[1, slot, :]
            probs = quotient.astype(jnp.bfloat16)
            dscores = (quotient * (dots - whole[2, slot, :])).astype(jnp.bfloat16)
            key_part = jnp.dot(dscores, queries, preferred_element_type=jnp.float32)
            value_part = jnp.dot(probs, grads, preferred_element_type=jnp.float32)
            if other == 0 and head == 0:
                key_sum[...] = key_part
                value_sum[...] = value_part
            else:
                key_sum[...] += key_part
                value_sum[...] += value_part
    out[:, :HEAD] = (key_sum[...] * SCALE).astype(jnp.bfloat16)
    out[:, HEAD:] = value_sum[...].astype(jnp.bfloat16)


def arrange_kernel(
    place, weight, hidden, queries, grads, turned, own, pair, blocks, both, arrived, left
):
    width = own.shape[1] // 4
    columns = [pl.ds(part * width, width) for part in range(4)]
    moves = [
        (weight.at[:, pl.ds((part * 8 + member) * width, width)], blocks.at[member, :, columns[part]])
        for member in range(8)
        for part in range(4)
    ]
    for part in range(4):
        start = pl.multiple_of((part * 8 + place[0]) * width, width)
        moves.append((hidden.at[:, pl.ds(start, width)], own.at[:, columns[part]]))
    moves += [(queries, both.at[0]), (grads, both.at[1])]
    copies = fetch(moves, arrived)
    sent = [
        pltpu.make_async_copy(blocks.at[member], turned.at[member], left.at[member])
        for member in range(8)
    ]
    sent += [pltpu.make_async_copy(both.at[kind], pair.at[kind], left.at[8 + kind]) for kind in range(2)]
    for member in range(8):
        for copy in copies[4 * member : 4 * member + 4]:
            copy.wait()
        sent[member].start()
    for kind in range(2):
        copies[36 + kind].wait()
        sent[8 + kind].start()
    for copy in copies[32:36] + sent:
        copy.wait()


def repeat_kernel(block, out):
    for index in range(out.shape[0]):
        out[index] = block[...]


def project_kernel(states, heads, out):
    for head in range(2):
        product = lax.dot_general(
            states[...], heads[head], NT, preferred_element_type=jnp.float32
        ).astype(jnp.bfloat16)
        for quarter in range(4):
            out[head * 4 + quarter] = product[quarter * TOKENS : (quarter + 1) * TOKENS]


def hidden_kernel(kv_grads, heads, out, parts, sems):
    copies = []
    for quarter in range(4):
        rows = pl.ds(quarter * TOKENS, TOKENS)
        parts[quarter] = (
            jnp.dot(kv_grads[0, rows, :], heads[0], preferred_element_type=jnp.float32)
            + jnp.dot(kv_grads[1, rows, :], heads[1], preferred_element_type=jnp.float32)
        ).astype(jnp.bfloat16)
        copy = pltpu.make_async_copy(parts.at[quarter], out.at[quarter], sems.at[quarter])
        copy.start()
        copies.append(copy)
    for copy in copies:
        copy.wait()


def weight_kernel(place, kv_grads, states, mine, one, three, rows):
    for head in range(2):
        rows[head * 256 : (head + 1) * 256, :] = lax.dot_general(
            kv_grads[head],
            states[...],
            (((0,), (0,)), ((), ())),
            preferred_element_type=jnp.float32,
        ).astype(jnp.bfloat16)

    def block(chip, core, start, count):
        first = ((place[0] // 2) ^ chip) * 128 + core * 64 + start
        return rows[pl.ds(pl.multiple_of(first, 32), count), :]

    for core in range(2):
        mine[core] = block(0, core, 0, 64)
        one[core, :64] = block(1, core, 0, 64)
        one[core, 64:] = block(2, core, 0, 32)
        three[core, :64] = block(3, core, 0, 64)
        three[core, 64:] = block(2, core, 32, 32)


def cores_kernel(place, mine, one, three, upper, lower, kept, passed):
    for out, core in ((kept, place[0] % 2), (passed, 1 - place[0] % 2)):
        out[0] = mine[core]
        out[1] = one[core, :64]
        out[2, :32] = upper[core]
        out[2, 32:] = lower[core]
        out[3] = three[core, :64]


def place_kernel(place, kept, taken, out):
    width = kept.shape[2] // 4
    for chip in range(4):
        for core, blocks in enumerate((kept, taken)):
            for part in range(4):
                member = place[0] ^ (chip * 2 + core)
                start = pl.multiple_of((part * 8 + member) * width, width)
                out[0, :, pl.ds(start, width)] = blocks[
                    chip, :, part * width : (part + 1) * width
                ].astype(jnp.float32)


def reduce_x_kernel(blocks, out):
    width = blocks.shape[2] // 4
    for high in range(4):
        rows = pl.ds(high * 32, 32)
        total = blocks[0, rows, :].astype(jnp.float32)
        for source in range(1, 4):
            total = total + blocks[source, rows, :].astype(jnp.float32)
        total = total.astype(jnp.bfloat16)
        for low in range(4):
            out[high * 4 + low] = total[:, low * width : (low + 1) * width]


def called(
    kernel, out_shape, operands, flops, moved, scratch=(), places=(), outs=None, limit=16, grid=()
):
    vmem = pl.BlockSpec(memory_space=pltpu.VMEM)
    return pl.pallas_call(
        kernel,
        grid=grid,
        out_shape=out_shape,
        in_specs=list(places) + [vmem] * (len(operands) - len(places)),
        out_specs=jax.tree.map(lambda leaf: vmem, out_shape) if outs is None else outs,
        scratch_shapes=list(scratch),
        compiler_params=pltpu.CompilerParams(vmem_limit_bytes=limit * 1024 * 1024),
        cost_estimate=pl.CostEstimate(
            flops=flops, bytes_accessed=moved, transcendentals=flops // 512
        ),
    )(*operands)


def shaped(dtype, *shape):
    return jax.ShapeDtypeStruct(shape, dtype)


def shards(hidden, kv_weight, queries, out_grads, cache, prefix_len, doc_start):
    plane_rank = lax.axis_index(PLANE)
    rank = lax.axis_index(QUAD)
    member = jnp.reshape(plane_rank, (1,)).astype(jnp.int32)
    place = jnp.reshape(rank, (1,)).astype(jnp.int32)
    width = hidden.shape[1] // 8
    bf16 = jnp.bfloat16
    f32 = jnp.float32
    smem = pl.BlockSpec(memory_space=pltpu.SMEM)
    vmem = pl.BlockSpec(memory_space=pltpu.VMEM)
    anywhere = pl.BlockSpec(memory_space=pl.ANY)
    hbm = pl.BlockSpec(memory_space=pltpu.HBM)
    dma = pltpu.SemaphoreType.DMA

    def far(value):
        return pltpu.with_memory_space_constraint(value, pltpu.HBM)

    q0 = queries[0]
    o0 = out_grads[0]
    turned, own, pair = called(
        arrange_kernel,
        (shaped(bf16, 8, 64, width), shaped(bf16, 32, width), shaped(bf16, 2, R, 256)),
        (member, far(kv_weight[0]), far(hidden), far(q0), far(o0)),
        0,
        4 << 20,
        (
            pltpu.VMEM((8, 64, width), bf16),
            pltpu.VMEM((2, R, 256), bf16),
            dma((38,)),
            dma((10,)),
        ),
        (smem, hbm, hbm, hbm, hbm),
        (anywhere, vmem, anywhere),
    )
    turned = lax.all_to_all(turned, PLANE, 0, 0, tiled=True)

    own = lax.all_gather(own, "zh", axis=0, tiled=True)
    own, turned, pair, cached = lax.optimization_barrier((own, turned, pair, cache[0]))
    states = called(repeat_kernel, shaped(bf16, 4, 128, width), (own,), 0, 1 << 20)
    states = lax.all_to_all(states, "x", 0, 0, tiled=True)

    p2 = swapped(pair, QUAD, 2)
    beside = swapped(cached, QUAD, 1)
    p1 = swapped(pair, QUAD, 1)

    states = states.reshape(R, width)
    heads = turned.reshape(2, 256, width)
    partial = called(
        project_kernel,
        shaped(bf16, 8, TOKENS, 256),
        (states, heads),
        2 * R * 512 * width,
        3 << 20,
    )
    p2, partial = lax.optimization_barrier((p2, partial))
    p3 = swapped(p2, QUAD, 1)
    sources = (q0, o0, p1, p2, p3)
    before = called(
        prefix_kernel,
        shaped(f32, 3, 4, R),
        (place, prefix_len.reshape(1, R), cache[0], beside, q0, o0, p2),
        2 * 2 * 8 * R * POSITIONS * HEAD * 4,
        3 << 20,
        (),
        (smem,),
        limit=16,
    )
    partial = lax.all_to_all(partial, PLANE, 0, 0, tiled=True)

    starts = doc_start.reshape(1, R)
    stats, kv, pairs = called(
        new_stats_kernel,
        (shaped(f32, 3, 8, R), shaped(bf16, TOKENS, 256), shaped(bf16, 4, 2, R, 256)),
        (place, starts, before, partial, *(far(source) for source in sources)),
        2 * 2 * 8 * R * TOKENS * HEAD * 4,
        3 << 20,
        (dma((8,)),),
        (smem, vmem, vmem, vmem) + (hbm,) * 5,
    )
    every = lax.all_gather(stats, QUAD, axis=0)
    grads = called(
        new_grads_kernel,
        shaped(bf16, TOKENS, 256),
        (place, kv, pairs, starts, every),
        4 * 2 * 8 * R * TOKENS * HEAD * 4,
        3 << 20,
        (
            pltpu.VMEM((3, 8, R), f32),
            pltpu.VMEM((TOKENS, HEAD), f32),
            pltpu.VMEM((TOKENS, HEAD), f32),
        ),
        (smem,),
    )
    kv_grads = lax.all_gather(grads, PLANE, axis=0, tiled=True).reshape(2, R, 256)

    hidden_part = called(
        hidden_kernel,
        shaped(bf16, 4, TOKENS, width),
        (kv_grads, heads),
        2 * R * 512 * width,
        3 << 20,
        (pltpu.VMEM((4, TOKENS, width), bf16), dma((4,))),
        outs=anywhere,
    )
    hidden_part, kv_grads = lax.optimization_barrier((hidden_part, kv_grads))
    over_x = lax.all_to_all(hidden_part, "x", 0, 0, tiled=True)
    over_x = called(reduce_x_kernel, shaped(bf16, 16, 32, width // 4), (over_x,), 0, 1 << 20)

    mine, one, three = called(
        weight_kernel,
        (shaped(bf16, 2, 64, width),) + (shaped(bf16, 2, 96, width),) * 2,
        (member, kv_grads, states),
        2 * R * 512 * width,
        3 << 20,
        (pltpu.VMEM((512, width), bf16),),
        (smem,),
    )
    one = swapped(one, PLANE, 2)
    three = swapped(three, PLANE, 6)
    over_x, one = lax.optimization_barrier((over_x, one))
    over_z = lax.all_to_all(over_x, ("zh", "zl"), 0, 0, tiled=True)
    hidden_grads = jnp.sum(over_z.astype(f32), axis=0)

    upper = swapped(one[:, 64:], PLANE, 6)
    lower = swapped(three[:, 64:], PLANE, 2)
    kept, passed = called(
        cores_kernel,
        (shaped(bf16, 4, 64, width),) * 2,
        (member, mine, one, three, upper, lower),
        0,
        1 << 20,
        (),
        (smem,),
    )
    taken = swapped(passed, PLANE, 1)
    weight_grads = called(
        place_kernel,
        shaped(f32, 1, 64, 8 * width),
        (member, kept, taken),
        0,
        3 << 20,
        (),
        (smem,),
    )
    return hidden_grads, weight_grads


def solution(mesh):
    axes = ("zh", "x", "zl", "yh", "yl", "core")
    split = Mesh(mesh.devices.reshape(4, 4, 4, 2, 2, 2), axes)
    pipe = ("zh", "x")
    tensor = ("zl", "yh", "yl", "core")
    return jax.shard_map(
        shards,
        mesh=split,
        in_specs=(
            P(pipe, None),
            P(pipe, tensor, None),
            P(pipe, None, tensor),
            P(pipe, None, tensor),
            P(pipe, None, tensor, None),
            P(),
            P(),
        ),
        out_specs=(P(pipe, tensor), P(pipe, tensor, None)),
        check_vma=False,
    )
```

```python
import functools

import jax
import jax.numpy as jnp
from jax import lax
from jax.experimental import pallas as pl
from jax.experimental.pallas import tpu as pltpu
from jax.sharding import Mesh, PartitionSpec as P

HEAD = 128
R = 512
POSITIONS = 1024
TOKENS = 128
SCALE = HEAD**-0.5
LOG2E = 1.4426950408889634
LOW = -1e30
PLANE = ("yh", "yl", "core")
QUAD = ("yl", "core")
NT = (((1,), (1,)), ((), ()))


def swapped(value, axes, moved):
    count = 1
    for axis in axes:
        count *= lax.axis_size(axis)
    pairs = [(source, source ^ moved) for source in range(count)]
    return lax.ppermute(value, axes, pairs)


def softmax_parts(scores, dots):
    top = jnp.max(scores, axis=0, keepdims=True)
    weights = jnp.exp2((scores - top) * (SCALE * LOG2E))
    total = jnp.sum(weights, axis=0, keepdims=True)
    accum = jnp.sum(weights * dots, axis=0, keepdims=True)
    return top, total, accum


def merged(first, second):
    top = jnp.maximum(first[0], second[0])
    fade_first = jnp.exp2((first[0] - top) * (SCALE * LOG2E))
    fade_second = jnp.exp2((second[0] - top) * (SCALE * LOG2E))
    return (
        top,
        first[1] * fade_first + second[1] * fade_second,
        first[2] * fade_first + second[2] * fade_second,
    )


def fetch(moves, sems):
    copies = [
        pltpu.make_async_copy(source, target, sems.at[index])
        for index, (source, target) in enumerate(moves)
    ]
    for copy in copies:
        copy.start()
    return copies


def prefix_stats(rank, lengths, blocks_of, queries, grads):
    chunk = 512
    parts = None
    for core, blocks in blocks_of:
        for start in range(0, POSITIONS, chunk):
            rows = pl.ds(start, chunk)
            scores = lax.dot_general(
                blocks[0, rows, :], queries, NT, preferred_element_type=jnp.float32
            )
            dots = lax.dot_general(
                blocks[1, rows, :], grads, NT, preferred_element_type=jnp.float32
            )
            ids = lax.broadcasted_iota(jnp.int32, (chunk, R), 0)
            limit = lengths - ((rank ^ core) * POSITIONS + start)
            piece = softmax_parts(jnp.where(ids < limit, scores, LOW), dots)
            parts = piece if parts is None else merged(parts, piece)
    return parts


def first_prefix_kernel(place, prefix_len, cache, q0, o0, stats):
    for head in range(2):
        columns = pl.ds(head * HEAD, HEAD)
        parts = prefix_stats(
            place[0], prefix_len[...], ((0, cache),), q0[:, columns], o0[:, columns]
        )
        for kind in range(3):
            stats[kind, pl.ds(head, 1), :] = parts[kind]


def prefix_kernel(place, prefix_len, first, cache, beside, q0, o0, p2, stats):
    for slot in range(4):
        q, o = (q0, o0) if slot < 2 else (p2.at[0], p2.at[1])
        blocks_of = ((1, beside),) if slot < 2 else ((0, cache), (1, beside))
        columns = pl.ds(slot % 2 * HEAD, HEAD)
        parts = prefix_stats(
            place[0], prefix_len[...], blocks_of, q[:, columns], o[:, columns]
        )
        if slot < 2:
            parts = merged(parts, tuple(first[kind, pl.ds(slot, 1), :] for kind in range(3)))
        for kind in range(3):
            stats[kind, pl.ds(slot, 1), :] = parts[kind]


def new_scores(rank, doc_start, keys, values, queries, grads):
    scores = lax.dot_general(keys, queries, NT, preferred_element_type=jnp.float32)
    dots = lax.dot_general(values, grads, NT, preferred_element_type=jnp.float32)
    place = lax.broadcasted_iota(jnp.int32, (TOKENS, R), 0)
    token = (place // 32) * 128 + rank * 32 + place % 32
    row = lax.broadcasted_iota(jnp.int32, (TOKENS, R), 1)
    mask = (token >= doc_start) & (token <= row)
    return jnp.where(mask, scores, LOW), dots


def new_stats_kernel(
    place, doc_start, before, partial, q0, o0, p1, p2, p3, stats, kv, pairs, sems
):
    rank = place[0]
    sources = ((q0, o0), (p1.at[0], p1.at[1]), (p2.at[0], p2.at[1]), (p3.at[0], p3.at[1]))
    copies = fetch(
        [
            (part, pairs.at[other, kind])
            for other, source in enumerate(sources)
            for kind, part in enumerate(source)
        ],
        sems,
    )
    total_kv = partial[0].astype(jnp.float32)
    for source in range(1, 8):
        total_kv = total_kv + partial[source].astype(jnp.float32)
    kv[...] = total_kv.astype(jnp.bfloat16)
    starts = doc_start[...]
    for other in range(4):
        copies[2 * other].wait()
        copies[2 * other + 1].wait()
        for head in range(2):
            columns = pl.ds(head * HEAD, HEAD)
            scores, dots = new_scores(
                rank,
                starts,
                kv[:, :HEAD],
                kv[:, HEAD:],
                pairs[other, 0, :, columns],
                pairs[other, 1, :, columns],
            )
            parts = softmax_parts(scores, dots)
            if other % 2 == 0:
                held = pl.ds(other + head, 1)
                parts = merged(parts, tuple(before[kind, held, :] for kind in range(3)))
            slot = pl.ds((rank ^ other) * 2 + head, 1)
            for kind in range(3):
                stats[kind, slot, :] = parts[kind]


def new_grads_kernel(
    place, kv, pairs, doc_start, every, out, whole, key_sum, value_sum
):
    rank = place[0]
    top = jnp.maximum(
        jnp.maximum(every[0, 0], every[1, 0]), jnp.maximum(every[2, 0], every[3, 0])
    )
    total = jnp.zeros_like(top)
    accum = jnp.zeros_like(top)
    for member in range(4):
        fade = jnp.exp2((every[member, 0] - top) * (SCALE * LOG2E))
        total = total + every[member, 1] * fade
        accum = accum + every[member, 2] * fade
    whole[0] = top
    whole[1] = 1.0 / total
    whole[2] = accum / total
    starts = doc_start[...]
    for other in range(4):
        for head in range(2):
            columns = pl.ds(head * HEAD, HEAD)
            queries = pairs[other, 0, :, columns]
            grads = pairs[other, 1, :, columns]
            scores, dots = new_scores(
                rank, starts, kv[:, :HEAD], kv[:, HEAD:], queries, grads
            )
            slot = pl.ds((rank ^ other) * 2 + head, 1)
            quotient = jnp.exp2((scores - whole[0, slot, :]) * (SCALE * LOG2E)) * whole[1, slot, :]
            probs = quotient.astype(jnp.bfloat16)
            dscores = (quotient * (dots - whole[2, slot, :])).astype(jnp.bfloat16)
            key_part = jnp.dot(dscores, queries, preferred_element_type=jnp.float32)
            value_part = jnp.dot(probs, grads, preferred_element_type=jnp.float32)
            if other == 0 and head == 0:
                key_sum[...] = key_part
                value_sum[...] = value_part
            else:
                key_sum[...] += key_part
                value_sum[...] += value_part
    out[:, :HEAD] = (key_sum[...] * SCALE).astype(jnp.bfloat16)
    out[:, HEAD:] = value_sum[...].astype(jnp.bfloat16)


def arrange_kernel(place, weight, hidden, turned, own, blocks, arrived, left):
    width = own.shape[1] // 4
    columns = [pl.ds(part * width, width) for part in range(4)]
    moves = [
        (weight.at[:, pl.ds((part * 8 + member) * width, width)], blocks.at[member, :, columns[part]])
        for member in range(8)
        for part in range(4)
    ]
    for part in range(4):
        start = pl.multiple_of((part * 8 + place[0]) * width, width)
        moves.append((hidden.at[:, pl.ds(start, width)], own.at[:, columns[part]]))
    copies = fetch(moves, arrived)
    sent = [
        pltpu.make_async_copy(blocks.at[member], turned.at[member], left.at[member])
        for member in range(8)
    ]
    for member in range(8):
        for copy in copies[4 * member : 4 * member + 4]:
            copy.wait()
        sent[member].start()
    for copy in copies[32:] + sent:
        copy.wait()


def pair_kernel(queries, grads, pair):
    pair[0] = queries[...]
    pair[1] = grads[...]


def repeat_kernel(block, out):
    for index in range(out.shape[0]):
        out[index] = block[...]


def project_kernel(states, heads, out):
    for head in range(2):
        product = lax.dot_general(
            states[...], heads[head], NT, preferred_element_type=jnp.float32
        ).astype(jnp.bfloat16)
        for quarter in range(4):
            out[head * 4 + quarter] = product[quarter * TOKENS : (quarter + 1) * TOKENS]


def hidden_kernel(kv_grads, heads, out, parts, sems):
    copies = []
    for quarter in range(4):
        rows = pl.ds(quarter * TOKENS, TOKENS)
        parts[quarter] = (
            jnp.dot(kv_grads[0, rows, :], heads[0], preferred_element_type=jnp.float32)
            + jnp.dot(kv_grads[1, rows, :], heads[1], preferred_element_type=jnp.float32)
        ).astype(jnp.bfloat16)
        copy = pltpu.make_async_copy(parts.at[quarter], out.at[quarter], sems.at[quarter])
        copy.start()
        copies.append(copy)
    for copy in copies:
        copy.wait()


def weight_kernel(place, kv_grads, states, mine, one, three, rows):
    for head in range(2):
        rows[head * 256 : (head + 1) * 256, :] = lax.dot_general(
            kv_grads[head],
            states[...],
            (((0,), (0,)), ((), ())),
            preferred_element_type=jnp.float32,
        ).astype(jnp.bfloat16)

    def block(chip, core, start, count):
        first = ((place[0] // 2) ^ chip) * 128 + core * 64 + start
        return rows[pl.ds(pl.multiple_of(first, 32), count), :]

    for core in range(2):
        mine[core] = block(0, core, 0, 64)
        one[core, :64] = block(1, core, 0, 64)
        one[core, 64:] = block(2, core, 0, 32)
        three[core, :64] = block(3, core, 0, 64)
        three[core, 64:] = block(2, core, 32, 32)


def cores_kernel(place, mine, one, three, upper, lower, kept, passed):
    for out, core in ((kept, place[0] % 2), (passed, 1 - place[0] % 2)):
        out[0] = mine[core]
        out[1] = one[core, :64]
        out[2, :32] = upper[core]
        out[2, 32:] = lower[core]
        out[3] = three[core, :64]


def place_kernel(place, kept, taken, out):
    width = kept.shape[2] // 4
    for chip in range(4):
        for core, blocks in enumerate((kept, taken)):
            for part in range(4):
                member = place[0] ^ (chip * 2 + core)
                start = pl.multiple_of((part * 8 + member) * width, width)
                out[0, :, pl.ds(start, width)] = blocks[
                    chip, :, part * width : (part + 1) * width
                ].astype(jnp.float32)


def reduce_x_kernel(blocks, out, sums, sems):
    width = blocks.shape[2] // 4
    copies = []
    for high in range(4):
        rows = pl.ds(high * 32, 32)
        total = blocks[0, rows, :].astype(jnp.float32)
        for source in range(1, 4):
            total = total + blocks[source, rows, :].astype(jnp.float32)
        total = total.astype(jnp.bfloat16)
        for low in range(4):
            sums[high * 4 + low] = total[:, low * width : (low + 1) * width]
        quarter = pl.ds(high * 4, 4)
        copy = pltpu.make_async_copy(sums.at[quarter], out.at[quarter], sems.at[high])
        copy.start()
        copies.append(copy)
    for copy in copies:
        copy.wait()


def called(
    kernel, out_shape, operands, flops, moved, scratch=(), places=(), outs=None, limit=16, grid=()
):
    vmem = pl.BlockSpec(memory_space=pltpu.VMEM)
    return pl.pallas_call(
        kernel,
        grid=grid,
        out_shape=out_shape,
        in_specs=list(places) + [vmem] * (len(operands) - len(places)),
        out_specs=jax.tree.map(lambda leaf: vmem, out_shape) if outs is None else outs,
        scratch_shapes=list(scratch),
        compiler_params=pltpu.CompilerParams(vmem_limit_bytes=limit * 1024 * 1024),
        cost_estimate=pl.CostEstimate(
            flops=flops, bytes_accessed=moved, transcendentals=flops // 512
        ),
    )(*operands)


def shaped(dtype, *shape):
    return jax.ShapeDtypeStruct(shape, dtype)


def shards(hidden, kv_weight, queries, out_grads, cache, prefix_len, doc_start):
    plane_rank = lax.axis_index(PLANE)
    rank = lax.axis_index(QUAD)
    member = jnp.reshape(plane_rank, (1,)).astype(jnp.int32)
    place = jnp.reshape(rank, (1,)).astype(jnp.int32)
    width = hidden.shape[1] // 8
    bf16 = jnp.bfloat16
    f32 = jnp.float32
    smem = pl.BlockSpec(memory_space=pltpu.SMEM)
    vmem = pl.BlockSpec(memory_space=pltpu.VMEM)
    anywhere = pl.BlockSpec(memory_space=pl.ANY)
    hbm = pl.BlockSpec(memory_space=pltpu.HBM)
    dma = pltpu.SemaphoreType.DMA

    def far(value):
        return pltpu.with_memory_space_constraint(value, pltpu.HBM)

    q0 = queries[0]
    o0 = out_grads[0]
    turned, own = called(
        arrange_kernel,
        (shaped(bf16, 8, 64, width), shaped(bf16, 32, width)),
        (member, far(kv_weight[0]), far(hidden)),
        0,
        4 << 20,
        (pltpu.VMEM((8, 64, width), bf16), dma((36,)), dma((8,))),
        (smem, hbm, hbm),
        (anywhere, vmem),
    )

    turned = lax.all_to_all(turned, PLANE, 0, 0, tiled=True)

    own = lax.all_gather(own, "zh", axis=0, tiled=True)
    own, turned, cached = lax.optimization_barrier((own, turned, cache[0]))
    states = called(repeat_kernel, shaped(bf16, 4, 128, width), (own,), 0, 1 << 20)
    states, sent_q, sent_o = lax.optimization_barrier((states, q0, o0))
    pair = called(pair_kernel, shaped(bf16, 2, R, 256), (sent_q, sent_o), 0, 1 << 16)
    states = lax.all_to_all(states, "x", 0, 0, tiled=True)

    p2 = swapped(pair, QUAD, 2)
    beside = swapped(cached, QUAD, 1)
    p1 = swapped(pair, QUAD, 1)
    lengths = prefix_len.reshape(1, R)
    first = called(
        first_prefix_kernel,
        shaped(f32, 3, 2, R),
        (place, lengths, far(cache[0]), far(q0), far(o0)),
        2 * 2 * 2 * R * POSITIONS * HEAD,
        1 << 20,
        (),
        (smem,),
        limit=16,
    )
    states, first = lax.optimization_barrier((states, first))

    states = states.reshape(R, width)
    heads = turned.reshape(2, 256, width)
    partial = called(
        project_kernel,
        shaped(bf16, 8, TOKENS, 256),
        (states, heads),
        2 * R * 512 * width,
        3 << 20,
    )
    p2, partial = lax.optimization_barrier((p2, partial))
    p3 = swapped(p2, QUAD, 1)
    sources = (q0, o0, p1, p2, p3)
    before = called(
        prefix_kernel,
        shaped(f32, 3, 4, R),
        (place, lengths, first, far(cache[0]), beside, far(q0), far(o0), p2),
        2 * 2 * 8 * R * POSITIONS * HEAD * 4,
        3 << 20,
        (),
        (smem,),
        limit=16,
    )
    partial = lax.all_to_all(partial, PLANE, 0, 0, tiled=True)

    starts = doc_start.reshape(1, R)
    stats, kv, pairs = called(
        new_stats_kernel,
        (shaped(f32, 3, 8, R), shaped(bf16, TOKENS, 256), shaped(bf16, 4, 2, R, 256)),
        (place, starts, before, partial, *(far(source) for source in sources)),
        2 * 2 * 8 * R * TOKENS * HEAD * 4,
        3 << 20,
        (dma((8,)),),
        (smem, vmem, vmem, vmem) + (hbm,) * 5,
    )
    every = lax.all_gather(stats, QUAD, axis=0)
    grads = called(
        new_grads_kernel,
        shaped(bf16, TOKENS, 256),
        (place, kv, pairs, starts, every),
        4 * 2 * 8 * R * TOKENS * HEAD * 4,
        3 << 20,
        (
            pltpu.VMEM((3, 8, R), f32),
            pltpu.VMEM((TOKENS, HEAD), f32),
            pltpu.VMEM((TOKENS, HEAD), f32),
        ),
        (smem,),
    )
    kv_grads = lax.all_gather(grads, PLANE, axis=0, tiled=True).reshape(2, R, 256)

    hidden_part = called(
        hidden_kernel,
        shaped(bf16, 4, TOKENS, width),
        (kv_grads, heads),
        2 * R * 512 * width,
        3 << 20,
        (pltpu.VMEM((4, TOKENS, width), bf16), dma((4,))),
        outs=anywhere,
    )
    hidden_part, kv_grads = lax.optimization_barrier((hidden_part, kv_grads))
    over_x = lax.all_to_all(hidden_part, "x", 0, 0, tiled=True)
    over_x = called(
        reduce_x_kernel,
        shaped(bf16, 16, 32, width // 4),
        (over_x,),
        0,
        1 << 20,
        (pltpu.VMEM((16, 32, width // 4), bf16), dma((4,))),
        outs=anywhere,
    )

    mine, one, three = called(
        weight_kernel,
        (shaped(bf16, 2, 64, width),) + (shaped(bf16, 2, 96, width),) * 2,
        (member, kv_grads, states),
        2 * R * 512 * width,
        3 << 20,
        (pltpu.VMEM((512, width), bf16),),
        (smem,),
    )
    one = swapped(one, PLANE, 2)
    three = swapped(three, PLANE, 6)
    over_x, one = lax.optimization_barrier((over_x, one))
    over_z = lax.all_to_all(over_x, ("zh", "zl"), 0, 0, tiled=True)
    hidden_grads = jnp.sum(over_z.astype(f32), axis=0)

    upper = swapped(one[:, 64:], PLANE, 6)
    lower = swapped(three[:, 64:], PLANE, 2)
    kept, passed = called(
        cores_kernel,
        (shaped(bf16, 4, 64, width),) * 2,
        (member, mine, one, three, upper, lower),
        0,
        1 << 20,
        (),
        (smem,),
    )
    taken = swapped(passed, PLANE, 1)
    weight_grads = called(
        place_kernel,
        shaped(f32, 1, 64, 8 * width),
        (member, kept, taken),
        0,
        3 << 20,
        (),
        (smem,),
    )
    return hidden_grads, weight_grads


def solution(mesh):
    axes = ("zh", "x", "zl", "yh", "yl", "core")
    split = Mesh(mesh.devices.reshape(4, 4, 4, 2, 2, 2), axes)
    pipe = ("zh", "x")
    tensor = ("zl", "yh", "yl", "core")
    return jax.shard_map(
        shards,
        mesh=split,
        in_specs=(
            P(pipe, None),
            P(pipe, tensor, None),
            P(pipe, None, tensor),
            P(pipe, None, tensor),
            P(pipe, None, tensor, None),
            P(),
            P(),
        ),
        out_specs=(P(pipe, tensor), P(pipe, tensor, None)),
        check_vma=False,
    )
```

```python
import functools

import jax
import jax.numpy as jnp
from jax import lax
from jax.experimental import pallas as pl
from jax.experimental.pallas import tpu as pltpu
from jax.sharding import Mesh, PartitionSpec as P

HEAD = 128
R = 512
POSITIONS = 1024
TOKENS = 128
SCALE = HEAD**-0.5
LOG2E = 1.4426950408889634
LOW = -1e30
SPREAD = 128.0
PLANE = ("yh", "yl", "core")
QUAD = ("yl", "core")
NT = (((1,), (1,)), ((), ()))


def swapped(value, axes, moved):
    count = 1
    for axis in axes:
        count *= lax.axis_size(axis)
    pairs = [(source, source ^ moved) for source in range(count)]
    return lax.ppermute(value, axes, pairs)


def softmax_parts(scores, dots):
    top = jnp.max(scores, axis=0, keepdims=True)
    weights = jnp.exp2((scores - top) * (SCALE * LOG2E))
    total = jnp.sum(weights, axis=0, keepdims=True)
    accum = jnp.sum(weights * dots, axis=0, keepdims=True)
    return top, total, accum


def merged(first, second):
    top = jnp.maximum(first[0], second[0])
    fade_first = jnp.exp2((first[0] - top) * (SCALE * LOG2E))
    fade_second = jnp.exp2((second[0] - top) * (SCALE * LOG2E))
    return (
        top,
        first[1] * fade_first + second[1] * fade_second,
        first[2] * fade_first + second[2] * fade_second,
    )


def fetch(moves, sems):
    copies = [
        pltpu.make_async_copy(source, target, sems.at[index])
        for index, (source, target) in enumerate(moves)
    ]
    for copy in copies:
        copy.start()
    return copies


def prefix_stats(rank, lengths, blocks_of, queries, grads):
    chunk = 512
    parts = None
    for core, blocks in blocks_of:
        for start in range(0, POSITIONS, chunk):
            rows = pl.ds(start, chunk)
            scores = lax.dot_general(
                blocks[0, rows, :], queries, NT, preferred_element_type=jnp.float32
            )
            dots = lax.dot_general(
                blocks[1, rows, :], grads, NT, preferred_element_type=jnp.float32
            )
            ids = lax.broadcasted_iota(jnp.int32, (chunk, R), 0)
            limit = lengths - ((rank ^ core) * POSITIONS + start)
            piece = softmax_parts(jnp.where(ids < limit, scores, LOW), dots)
            parts = piece if parts is None else merged(parts, piece)
    return parts


def first_prefix_kernel(place, prefix_len, cache, q0, o0, stats):
    for head in range(2):
        columns = pl.ds(head * HEAD, HEAD)
        parts = prefix_stats(
            place[0], prefix_len[...], ((0, cache),), q0[:, columns], o0[:, columns]
        )
        for kind in range(3):
            stats[kind, pl.ds(head, 1), :] = parts[kind]


def prefix_kernel(place, prefix_len, first, cache, beside, q0, o0, p2, stats):
    for slot in range(4):
        q, o = (q0, o0) if slot < 2 else (p2.at[0], p2.at[1])
        blocks_of = ((1, beside),) if slot < 2 else ((0, cache), (1, beside))
        columns = pl.ds(slot % 2 * HEAD, HEAD)
        parts = prefix_stats(
            place[0], prefix_len[...], blocks_of, q[:, columns], o[:, columns]
        )
        if slot < 2:
            parts = merged(parts, tuple(first[kind, pl.ds(slot, 1), :] for kind in range(3)))
        for kind in range(3):
            stats[kind, pl.ds(slot, 1), :] = parts[kind]


def new_scores(rank, doc_start, keys, values, queries, grads):
    scores = lax.dot_general(keys, queries, NT, preferred_element_type=jnp.float32)
    dots = lax.dot_general(values, grads, NT, preferred_element_type=jnp.float32)
    place = lax.broadcasted_iota(jnp.int32, (TOKENS, R), 0)
    token = (place // 32) * 128 + rank * 32 + place % 32
    row = lax.broadcasted_iota(jnp.int32, (TOKENS, R), 1)
    mask = (token >= doc_start) & (token <= row)
    return jnp.where(mask, scores, LOW), dots


def new_stats_kernel(
    place, doc_start, before, kv, q0, o0, p1, p2, p3, stats, pairs, sems
):
    rank = place[0]
    sources = ((q0, o0), (p1.at[0], p1.at[1]), (p2.at[0], p2.at[1]), (p3.at[0], p3.at[1]))
    copies = fetch(
        [
            (part, pairs.at[other, kind])
            for other, source in enumerate(sources)
            for kind, part in enumerate(source)
        ],
        sems,
    )
    starts = doc_start[...]
    for other in range(4):
        copies[2 * other].wait()
        copies[2 * other + 1].wait()
        for head in range(2):
            columns = pl.ds(head * HEAD, HEAD)
            scores, dots = new_scores(
                rank,
                starts,
                kv[:, :HEAD],
                kv[:, HEAD:],
                pairs[other, 0, :, columns],
                pairs[other, 1, :, columns],
            )
            parts = softmax_parts(scores, dots)
            if other % 2 == 0:
                held = pl.ds(other + head, 1)
                parts = merged(parts, tuple(before[kind, held, :] for kind in range(3)))
            slot = pl.ds((rank ^ other) * 2 + head, 1)
            for kind in range(3):
                stats[kind, slot, :] = parts[kind]


def new_grads_kernel(
    place, kv, pairs, doc_start, every, out, whole, key_sum, value_sum
):
    rank = place[0]
    top = jnp.maximum(
        jnp.maximum(every[0, 0], every[1, 0]), jnp.maximum(every[2, 0], every[3, 0])
    )
    total = jnp.zeros_like(top)
    accum = jnp.zeros_like(top)
    for member in range(4):
        fade = jnp.exp2((every[member, 0] - top) * (SCALE * LOG2E))
        total = total + every[member, 1] * fade
        accum = accum + every[member, 2] * fade
    whole[0] = top
    whole[1] = 1.0 / total
    whole[2] = accum / total
    starts = doc_start[...]
    for other in range(4):
        for head in range(2):
            columns = pl.ds(head * HEAD, HEAD)
            queries = pairs[other, 0, :, columns]
            grads = pairs[other, 1, :, columns]
            scores, dots = new_scores(
                rank, starts, kv[:, :HEAD], kv[:, HEAD:], queries, grads
            )
            slot = pl.ds((rank ^ other) * 2 + head, 1)
            quotient = jnp.exp2((scores - whole[0, slot, :]) * (SCALE * LOG2E)) * whole[1, slot, :]
            probs = quotient.astype(jnp.bfloat16)
            dscores = (quotient * (dots - whole[2, slot, :])).astype(jnp.bfloat16)
            key_part = jnp.dot(dscores, queries, preferred_element_type=jnp.float32)
            value_part = jnp.dot(probs, grads, preferred_element_type=jnp.float32)
            if other == 0 and head == 0:
                key_sum[...] = key_part
                value_sum[...] = value_part
            else:
                key_sum[...] += key_part
                value_sum[...] += value_part
    out[:, :HEAD] = (key_sum[...] * SCALE).astype(jnp.bfloat16)
    out[:, HEAD:] = value_sum[...].astype(jnp.bfloat16)


def arrange_kernel(place, weight, hidden, turned, own, blocks, arrived, left):
    width = own.shape[1] // 4
    columns = [pl.ds(part * width, width) for part in range(4)]
    moves = [
        (weight.at[:, pl.ds((part * 8 + member) * width, width)], blocks.at[member, :, columns[part]])
        for member in range(8)
        for part in range(4)
    ]
    for part in range(4):
        start = pl.multiple_of((part * 8 + place[0]) * width, width)
        moves.append((hidden.at[:, pl.ds(start, width)], own.at[:, columns[part]]))
    copies = fetch(moves, arrived)
    sent = [
        pltpu.make_async_copy(blocks.at[member], turned.at[member], left.at[member])
        for member in range(8)
    ]
    for member in range(8):
        for copy in copies[4 * member : 4 * member + 4]:
            copy.wait()
        sent[member].start()
    for copy in copies[32:] + sent:
        copy.wait()


def pair_kernel(queries, grads, pair):
    pair[0] = queries[...]
    pair[1] = grads[...]


def repeat_kernel(block, out):
    for index in range(out.shape[0]):
        out[index] = block[...]


def project_kernel(states, heads, out):
    for head in range(2):
        product = lax.dot_general(
            states[...], heads[head], NT, preferred_element_type=jnp.float32
        )
        product = product * SPREAD
        for quarter in range(4):
            out[head * 4 + quarter] = product[quarter * TOKENS : (quarter + 1) * TOKENS]


def hidden_kernel(kv_grads, heads, out, parts, sems):
    copies = []
    for quarter in range(4):
        rows = pl.ds(quarter * TOKENS, TOKENS)
        parts[quarter] = (
            jnp.dot(kv_grads[0, rows, :], heads[0], preferred_element_type=jnp.float32)
            + jnp.dot(kv_grads[1, rows, :], heads[1], preferred_element_type=jnp.float32)
        ).astype(jnp.bfloat16)
        copy = pltpu.make_async_copy(parts.at[quarter], out.at[quarter], sems.at[quarter])
        copy.start()
        copies.append(copy)
    for copy in copies:
        copy.wait()


def weight_kernel(place, kv_grads, states, mine, one, three, rows):
    for head in range(2):
        rows[head * 256 : (head + 1) * 256, :] = lax.dot_general(
            kv_grads[head],
            states[...],
            (((0,), (0,)), ((), ())),
            preferred_element_type=jnp.float32,
        ).astype(jnp.bfloat16)

    def block(chip, core, start, count):
        first = ((place[0] // 2) ^ chip) * 128 + core * 64 + start
        return rows[pl.ds(pl.multiple_of(first, 32), count), :]

    for core in range(2):
        mine[core] = block(0, core, 0, 64)
        one[core, :64] = block(1, core, 0, 64)
        one[core, 64:] = block(2, core, 0, 32)
        three[core, :64] = block(3, core, 0, 64)
        three[core, 64:] = block(2, core, 32, 32)


def cores_kernel(place, mine, one, three, upper, lower, kept, passed):
    for out, core in ((kept, place[0] % 2), (passed, 1 - place[0] % 2)):
        out[0] = mine[core]
        out[1] = one[core, :64]
        out[2, :32] = upper[core]
        out[2, 32:] = lower[core]
        out[3] = three[core, :64]


def place_kernel(place, kept, taken, out):
    width = kept.shape[2] // 4
    for chip in range(4):
        for core, blocks in enumerate((kept, taken)):
            for part in range(4):
                member = place[0] ^ (chip * 2 + core)
                start = pl.multiple_of((part * 8 + member) * width, width)
                out[0, :, pl.ds(start, width)] = blocks[
                    chip, :, part * width : (part + 1) * width
                ].astype(jnp.float32)


def reduce_x_kernel(blocks, out, sums, sems):
    width = blocks.shape[2] // 4
    copies = []
    for high in range(4):
        rows = pl.ds(high * 32, 32)
        total = blocks[0, rows, :].astype(jnp.float32)
        for source in range(1, 4):
            total = total + blocks[source, rows, :].astype(jnp.float32)
        total = total.astype(jnp.bfloat16)
        for low in range(4):
            sums[high * 4 + low] = total[:, low * width : (low + 1) * width]
        quarter = pl.ds(high * 4, 4)
        copy = pltpu.make_async_copy(sums.at[quarter], out.at[quarter], sems.at[high])
        copy.start()
        copies.append(copy)
    for copy in copies:
        copy.wait()


def called(
    kernel, out_shape, operands, flops, moved, scratch=(), places=(), outs=None, limit=16, grid=()
):
    vmem = pl.BlockSpec(memory_space=pltpu.VMEM)
    return pl.pallas_call(
        kernel,
        grid=grid,
        out_shape=out_shape,
        in_specs=list(places) + [vmem] * (len(operands) - len(places)),
        out_specs=jax.tree.map(lambda leaf: vmem, out_shape) if outs is None else outs,
        scratch_shapes=list(scratch),
        compiler_params=pltpu.CompilerParams(vmem_limit_bytes=limit * 1024 * 1024),
        cost_estimate=pl.CostEstimate(
            flops=flops, bytes_accessed=moved, transcendentals=flops // 512
        ),
    )(*operands)


def shaped(dtype, *shape):
    return jax.ShapeDtypeStruct(shape, dtype)


def shards(hidden, kv_weight, queries, out_grads, cache, prefix_len, doc_start):
    plane_rank = lax.axis_index(PLANE)
    rank = lax.axis_index(QUAD)
    member = jnp.reshape(plane_rank, (1,)).astype(jnp.int32)
    place = jnp.reshape(rank, (1,)).astype(jnp.int32)
    width = hidden.shape[1] // 8
    bf16 = jnp.bfloat16
    f32 = jnp.float32
    smem = pl.BlockSpec(memory_space=pltpu.SMEM)
    vmem = pl.BlockSpec(memory_space=pltpu.VMEM)
    anywhere = pl.BlockSpec(memory_space=pl.ANY)
    hbm = pl.BlockSpec(memory_space=pltpu.HBM)
    dma = pltpu.SemaphoreType.DMA

    def far(value):
        return pltpu.with_memory_space_constraint(value, pltpu.HBM)

    q0 = queries[0]
    o0 = out_grads[0]
    turned, own = called(
        arrange_kernel,
        (shaped(bf16, 8, 64, width), shaped(bf16, 32, width)),
        (member, far(kv_weight[0]), far(hidden)),
        0,
        4 << 20,
        (pltpu.VMEM((8, 64, width), bf16), dma((36,)), dma((8,))),
        (smem, hbm, hbm),
        (anywhere, vmem),
    )

    turned = lax.all_to_all(turned, PLANE, 0, 0, tiled=True)

    own = lax.all_gather(own, "zh", axis=0, tiled=True)
    own, turned, cached = lax.optimization_barrier((own, turned, cache[0]))
    states = called(repeat_kernel, shaped(bf16, 4, 128, width), (own,), 0, 1 << 20)
    states, sent_q, sent_o = lax.optimization_barrier((states, q0, o0))
    pair = called(pair_kernel, shaped(bf16, 2, R, 256), (sent_q, sent_o), 0, 1 << 16)
    states = lax.all_to_all(states, "x", 0, 0, tiled=True)

    p2 = swapped(pair, QUAD, 2)
    beside = swapped(cached, QUAD, 1)
    p1 = swapped(pair, QUAD, 1)
    lengths = prefix_len.reshape(1, R)
    first = called(
        first_prefix_kernel,
        shaped(f32, 3, 2, R),
        (place, lengths, far(cache[0]), far(q0), far(o0)),
        2 * 2 * 2 * R * POSITIONS * HEAD,
        1 << 20,
        (),
        (smem,),
        limit=16,
    )
    states, first = lax.optimization_barrier((states, first))

    states = states.reshape(R, width)
    heads = turned.reshape(2, 256, width)
    partial = called(
        project_kernel,
        shaped(f32, 8, TOKENS, 256),
        (states, heads),
        2 * R * 512 * width,
        3 << 20,
    )
    p2, partial = lax.optimization_barrier((p2, partial))
    p3 = swapped(p2, QUAD, 1)
    sources = (q0, o0, p1, p2, p3)
    before = called(
        prefix_kernel,
        shaped(f32, 3, 4, R),
        (place, lengths, first, far(cache[0]), beside, far(q0), far(o0), p2),
        2 * 2 * 8 * R * POSITIONS * HEAD * 4,
        3 << 20,
        (),
        (smem,),
        limit=16,
    )
    partial = lax.all_to_all(partial.astype(jnp.float16), PLANE, 0, 0, tiled=True)
    kv = (jnp.sum(partial.astype(f32), axis=0) * (1 / SPREAD)).astype(bf16)

    starts = doc_start.reshape(1, R)
    stats, pairs = called(
        new_stats_kernel,
        (shaped(f32, 3, 8, R), shaped(bf16, 4, 2, R, 256)),
        (place, starts, before, kv, *(far(source) for source in sources)),
        2 * 2 * 8 * R * TOKENS * HEAD * 4,
        3 << 20,
        (dma((8,)),),
        (smem, vmem, vmem, vmem) + (hbm,) * 5,
    )
    every = lax.all_gather(stats, QUAD, axis=0)
    grads = called(
        new_grads_kernel,
        shaped(bf16, TOKENS, 256),
        (place, kv, pairs, starts, every),
        4 * 2 * 8 * R * TOKENS * HEAD * 4,
        3 << 20,
        (
            pltpu.VMEM((3, 8, R), f32),
            pltpu.VMEM((TOKENS, HEAD), f32),
            pltpu.VMEM((TOKENS, HEAD), f32),
        ),
        (smem,),
    )
    kv_grads = lax.all_gather(grads, PLANE, axis=0, tiled=True).reshape(2, R, 256)

    hidden_part = called(
        hidden_kernel,
        shaped(bf16, 4, TOKENS, width),
        (kv_grads, heads),
        2 * R * 512 * width,
        3 << 20,
        (pltpu.VMEM((4, TOKENS, width), bf16), dma((4,))),
        outs=anywhere,
    )
    hidden_part, kv_grads = lax.optimization_barrier((hidden_part, kv_grads))
    over_x = lax.all_to_all(hidden_part, "x", 0, 0, tiled=True)
    over_x = called(
        reduce_x_kernel,
        shaped(bf16, 16, 32, width // 4),
        (over_x,),
        0,
        1 << 20,
        (pltpu.VMEM((16, 32, width // 4), bf16), dma((4,))),
        outs=anywhere,
    )

    mine, one, three = called(
        weight_kernel,
        (shaped(bf16, 2, 64, width),) + (shaped(bf16, 2, 96, width),) * 2,
        (member, kv_grads, states),
        2 * R * 512 * width,
        3 << 20,
        (pltpu.VMEM((512, width), bf16),),
        (smem,),
    )
    one = swapped(one, PLANE, 2)
    three = swapped(three, PLANE, 6)
    over_x, one = lax.optimization_barrier((over_x, one))
    over_z = lax.all_to_all(over_x, ("zh", "zl"), 0, 0, tiled=True)
    hidden_grads = jnp.sum(over_z.astype(f32), axis=0)

    upper = swapped(one[:, 64:], PLANE, 6)
    lower = swapped(three[:, 64:], PLANE, 2)
    kept, passed = called(
        cores_kernel,
        (shaped(bf16, 4, 64, width),) * 2,
        (member, mine, one, three, upper, lower),
        0,
        1 << 20,
        (),
        (smem,),
    )
    taken = swapped(passed, PLANE, 1)
    weight_grads = called(
        place_kernel,
        shaped(f32, 1, 64, 8 * width),
        (member, kept, taken),
        0,
        3 << 20,
        (),
        (smem,),
    )
    return hidden_grads, weight_grads


def solution(mesh):
    axes = ("zh", "x", "zl", "yh", "yl", "core")
    split = Mesh(mesh.devices.reshape(4, 4, 4, 2, 2, 2), axes)
    pipe = ("zh", "x")
    tensor = ("zl", "yh", "yl", "core")
    return jax.shard_map(
        shards,
        mesh=split,
        in_specs=(
            P(pipe, None),
            P(pipe, tensor, None),
            P(pipe, None, tensor),
            P(pipe, None, tensor),
            P(pipe, None, tensor, None),
            P(),
            P(),
        ),
        out_specs=(P(pipe, tensor), P(pipe, tensor, None)),
        check_vma=False,
    )
```

```python
import functools

import jax
import jax.numpy as jnp
from jax import lax
from jax.experimental import pallas as pl
from jax.experimental.pallas import tpu as pltpu
from jax.sharding import Mesh, PartitionSpec as P

HEAD = 128
R = 512
POSITIONS = 1024
TOKENS = 128
SCALE = HEAD**-0.5
LOG2E = 1.4426950408889634
LOW = -1e30
SPREAD = 128.0
PLANE = ("yh", "yl", "core")
QUAD = ("yl", "core")
NT = (((1,), (1,)), ((), ()))


def swapped(value, axes, moved):
    count = 1
    for axis in axes:
        count *= lax.axis_size(axis)
    pairs = [(source, source ^ moved) for source in range(count)]
    return lax.ppermute(value, axes, pairs)


def softmax_parts(scores, dots):
    top = jnp.max(scores, axis=0, keepdims=True)
    weights = jnp.exp2((scores - top) * (SCALE * LOG2E))
    total = jnp.sum(weights, axis=0, keepdims=True)
    accum = jnp.sum(weights * dots, axis=0, keepdims=True)
    return top, total, accum


def merged(first, second):
    top = jnp.maximum(first[0], second[0])
    fade_first = jnp.exp2((first[0] - top) * (SCALE * LOG2E))
    fade_second = jnp.exp2((second[0] - top) * (SCALE * LOG2E))
    return (
        top,
        first[1] * fade_first + second[1] * fade_second,
        first[2] * fade_first + second[2] * fade_second,
    )


def fetch(moves, sems):
    copies = [
        pltpu.make_async_copy(source, target, sems.at[index])
        for index, (source, target) in enumerate(moves)
    ]
    for copy in copies:
        copy.start()
    return copies


def prefix_stats(rank, lengths, blocks_of, queries, grads):
    chunk = 512
    parts = None
    for core, blocks in blocks_of:
        for start in range(0, POSITIONS, chunk):
            rows = pl.ds(start, chunk)
            scores = lax.dot_general(
                blocks[0, rows, :], queries, NT, preferred_element_type=jnp.float32
            )
            dots = lax.dot_general(
                blocks[1, rows, :], grads, NT, preferred_element_type=jnp.float32
            )
            ids = lax.broadcasted_iota(jnp.int32, (chunk, R), 0)
            limit = lengths - ((rank ^ core) * POSITIONS + start)
            piece = softmax_parts(jnp.where(ids < limit, scores, LOW), dots)
            parts = piece if parts is None else merged(parts, piece)
    return parts


def first_prefix_kernel(place, prefix_len, cache, q0, o0, stats):
    for head in range(2):
        columns = pl.ds(head * HEAD, HEAD)
        parts = prefix_stats(
            place[0], prefix_len[...], ((0, cache),), q0[:, columns], o0[:, columns]
        )
        for kind in range(3):
            stats[kind, pl.ds(head, 1), :] = parts[kind]


def prefix_kernel(place, prefix_len, first, cache, beside, q0, o0, p2, stats):
    for slot in range(4):
        q, o = (q0, o0) if slot < 2 else (p2.at[0], p2.at[1])
        blocks_of = ((1, beside),) if slot < 2 else ((0, cache), (1, beside))
        columns = pl.ds(slot % 2 * HEAD, HEAD)
        parts = prefix_stats(
            place[0], prefix_len[...], blocks_of, q[:, columns], o[:, columns]
        )
        if slot < 2:
            parts = merged(parts, tuple(first[kind, pl.ds(slot, 1), :] for kind in range(3)))
        for kind in range(3):
            stats[kind, pl.ds(slot, 1), :] = parts[kind]


def new_scores(rank, doc_start, keys, values, queries, grads):
    scores = lax.dot_general(keys, queries, NT, preferred_element_type=jnp.float32)
    dots = lax.dot_general(values, grads, NT, preferred_element_type=jnp.float32)
    place = lax.broadcasted_iota(jnp.int32, (TOKENS, R), 0)
    token = (place // 32) * 128 + rank * 32 + place % 32
    row = lax.broadcasted_iota(jnp.int32, (TOKENS, R), 1)
    mask = (token >= doc_start) & (token <= row)
    return jnp.where(mask, scores, LOW), dots


def new_stats_kernel(
    place, doc_start, before, kv, q0, o0, p1, p2, p3, stats, pairs, sems
):
    rank = place[0]
    sources = ((q0, o0), (p1.at[0], p1.at[1]), (p2.at[0], p2.at[1]), (p3.at[0], p3.at[1]))
    copies = fetch(
        [
            (part, pairs.at[other, kind])
            for other, source in enumerate(sources)
            for kind, part in enumerate(source)
        ],
        sems,
    )
    starts = doc_start[...]
    for other in range(4):
        copies[2 * other].wait()
        copies[2 * other + 1].wait()
        for head in range(2):
            columns = pl.ds(head * HEAD, HEAD)
            scores, dots = new_scores(
                rank,
                starts,
                kv[:, :HEAD],
                kv[:, HEAD:],
                pairs[other, 0, :, columns],
                pairs[other, 1, :, columns],
            )
            parts = softmax_parts(scores, dots)
            if other % 2 == 0:
                held = pl.ds(other + head, 1)
                parts = merged(parts, tuple(before[kind, held, :] for kind in range(3)))
            slot = pl.ds((rank ^ other) * 2 + head, 1)
            for kind in range(3):
                stats[kind, slot, :] = parts[kind]


def new_grads_kernel(
    place, kv, pairs, doc_start, every, out, whole, key_sum, value_sum
):
    rank = place[0]
    top = jnp.maximum(
        jnp.maximum(every[0, 0], every[1, 0]), jnp.maximum(every[2, 0], every[3, 0])
    )
    total = jnp.zeros_like(top)
    accum = jnp.zeros_like(top)
    for member in range(4):
        fade = jnp.exp2((every[member, 0] - top) * (SCALE * LOG2E))
        total = total + every[member, 1] * fade
        accum = accum + every[member, 2] * fade
    whole[0] = top
    whole[1] = 1.0 / total
    whole[2] = accum / total
    key_sum[...] = jnp.zeros_like(key_sum)
    value_sum[...] = jnp.zeros_like(value_sum)
    starts = doc_start[...]
    for other in range(4):
        for head in range(2):
            columns = pl.ds(head * HEAD, HEAD)
            queries = pairs[other, 0, :, columns]
            grads = pairs[other, 1, :, columns]
            slot = pl.ds((rank ^ other) * 2 + head, 1)
            stats_of = [whole[kind, slot, :] for kind in range(3)]
            for block in range(4):
                rows = slice(block * 128, block * 128 + 128)
                count = 32 * (block + 1)
                query = queries[rows]
                grad = grads[rows]
                scores = lax.dot_general(
                    kv[:count, :HEAD], query, NT, preferred_element_type=jnp.float32
                )
                dots = lax.dot_general(
                    kv[:count, HEAD:], grad, NT, preferred_element_type=jnp.float32
                )
                place_of = lax.broadcasted_iota(jnp.int32, (count, 128), 0)
                token = (place_of // 32) * 128 + rank * 32 + place_of % 32
                row = lax.broadcasted_iota(jnp.int32, (count, 128), 1) + block * 128
                mask = (token >= starts[:, rows]) & (token <= row)
                scores = jnp.where(mask, scores, LOW)
                top_of, inverse, mean = (value[:, rows] for value in stats_of)
                quotient = jnp.exp2((scores - top_of) * (SCALE * LOG2E)) * inverse
                probs = quotient.astype(jnp.bfloat16)
                dscores = (quotient * (dots - mean)).astype(jnp.bfloat16)
                key_sum[:count] += jnp.dot(dscores, query, preferred_element_type=jnp.float32)
                value_sum[:count] += jnp.dot(probs, grad, preferred_element_type=jnp.float32)
    out[:, :HEAD] = (key_sum[...] * SCALE).astype(jnp.bfloat16)
    out[:, HEAD:] = value_sum[...].astype(jnp.bfloat16)


def arrange_kernel(place, weight, hidden, turned, own, blocks, arrived, left):
    width = own.shape[1] // 4
    columns = [pl.ds(part * width, width) for part in range(4)]
    moves = [
        (weight.at[:, pl.ds((part * 8 + member) * width, width)], blocks.at[member, :, columns[part]])
        for member in range(8)
        for part in range(4)
    ]
    for part in range(4):
        start = pl.multiple_of((part * 8 + place[0]) * width, width)
        moves.append((hidden.at[:, pl.ds(start, width)], own.at[:, columns[part]]))
    copies = fetch(moves, arrived)
    sent = [
        pltpu.make_async_copy(blocks.at[member], turned.at[member], left.at[member])
        for member in range(8)
    ]
    for member in range(8):
        for copy in copies[4 * member : 4 * member + 4]:
            copy.wait()
        sent[member].start()
    for copy in copies[32:] + sent:
        copy.wait()


def pair_kernel(queries, grads, pair):
    pair[0] = queries[...]
    pair[1] = grads[...]


def repeat_kernel(block, out):
    for index in range(out.shape[0]):
        out[index] = block[...]


def project_kernel(states, heads, out):
    for head in range(2):
        product = lax.dot_general(
            states[...], heads[head], NT, preferred_element_type=jnp.float32
        )
        product = product * SPREAD
        for quarter in range(4):
            out[head * 4 + quarter] = product[quarter * TOKENS : (quarter + 1) * TOKENS]


def hidden_kernel(kv_grads, heads, out, parts, sems):
    copies = []
    for quarter in range(4):
        rows = pl.ds(quarter * TOKENS, TOKENS)
        parts[quarter] = (
            jnp.dot(kv_grads[0, rows, :], heads[0], preferred_element_type=jnp.float32)
            + jnp.dot(kv_grads[1, rows, :], heads[1], preferred_element_type=jnp.float32)
        ).astype(jnp.bfloat16)
        copy = pltpu.make_async_copy(parts.at[quarter], out.at[quarter], sems.at[quarter])
        copy.start()
        copies.append(copy)
    for copy in copies:
        copy.wait()


def weight_kernel(place, kv_grads, states, mine, one, three, rows):
    for head in range(2):
        rows[head * 256 : (head + 1) * 256, :] = lax.dot_general(
            kv_grads[head],
            states[...],
            (((0,), (0,)), ((), ())),
            preferred_element_type=jnp.float32,
        ).astype(jnp.bfloat16)

    def block(chip, core, start, count):
        first = ((place[0] // 2) ^ chip) * 128 + core * 64 + start
        return rows[pl.ds(pl.multiple_of(first, 32), count), :]

    for core in range(2):
        mine[core] = block(0, core, 0, 64)
        one[core, :64] = block(1, core, 0, 64)
        one[core, 64:] = block(2, core, 0, 32)
        three[core, :64] = block(3, core, 0, 64)
        three[core, 64:] = block(2, core, 32, 32)


def cores_kernel(place, mine, one, three, upper, lower, kept, passed):
    for out, core in ((kept, place[0] % 2), (passed, 1 - place[0] % 2)):
        out[0] = mine[core]
        out[1] = one[core, :64]
        out[2, :32] = upper[core]
        out[2, 32:] = lower[core]
        out[3] = three[core, :64]


def place_kernel(place, kept, taken, out):
    width = kept.shape[2] // 4
    for chip in range(4):
        for core, blocks in enumerate((kept, taken)):
            for part in range(4):
                member = place[0] ^ (chip * 2 + core)
                start = pl.multiple_of((part * 8 + member) * width, width)
                out[0, :, pl.ds(start, width)] = blocks[
                    chip, :, part * width : (part + 1) * width
                ].astype(jnp.float32)


def reduce_x_kernel(blocks, out, sums, sems):
    width = blocks.shape[2] // 4
    copies = []
    for high in range(4):
        rows = pl.ds(high * 32, 32)
        total = blocks[0, rows, :].astype(jnp.float32)
        for source in range(1, 4):
            total = total + blocks[source, rows, :].astype(jnp.float32)
        total = total.astype(jnp.bfloat16)
        for low in range(4):
            sums[high * 4 + low] = total[:, low * width : (low + 1) * width]
        quarter = pl.ds(high * 4, 4)
        copy = pltpu.make_async_copy(sums.at[quarter], out.at[quarter], sems.at[high])
        copy.start()
        copies.append(copy)
    for copy in copies:
        copy.wait()


def called(
    kernel, out_shape, operands, flops, moved, scratch=(), places=(), outs=None, limit=16, grid=()
):
    vmem = pl.BlockSpec(memory_space=pltpu.VMEM)
    return pl.pallas_call(
        kernel,
        grid=grid,
        out_shape=out_shape,
        in_specs=list(places) + [vmem] * (len(operands) - len(places)),
        out_specs=jax.tree.map(lambda leaf: vmem, out_shape) if outs is None else outs,
        scratch_shapes=list(scratch),
        compiler_params=pltpu.CompilerParams(vmem_limit_bytes=limit * 1024 * 1024),
        cost_estimate=pl.CostEstimate(
            flops=flops, bytes_accessed=moved, transcendentals=flops // 512
        ),
    )(*operands)


def shaped(dtype, *shape):
    return jax.ShapeDtypeStruct(shape, dtype)


def shards(hidden, kv_weight, queries, out_grads, cache, prefix_len, doc_start):
    plane_rank = lax.axis_index(PLANE)
    rank = lax.axis_index(QUAD)
    member = jnp.reshape(plane_rank, (1,)).astype(jnp.int32)
    place = jnp.reshape(rank, (1,)).astype(jnp.int32)
    width = hidden.shape[1] // 8
    bf16 = jnp.bfloat16
    f32 = jnp.float32
    smem = pl.BlockSpec(memory_space=pltpu.SMEM)
    vmem = pl.BlockSpec(memory_space=pltpu.VMEM)
    anywhere = pl.BlockSpec(memory_space=pl.ANY)
    hbm = pl.BlockSpec(memory_space=pltpu.HBM)
    dma = pltpu.SemaphoreType.DMA

    def far(value):
        return pltpu.with_memory_space_constraint(value, pltpu.HBM)

    q0 = queries[0]
    o0 = out_grads[0]
    turned, own = called(
        arrange_kernel,
        (shaped(bf16, 8, 64, width), shaped(bf16, 32, width)),
        (member, far(kv_weight[0]), far(hidden)),
        0,
        4 << 20,
        (pltpu.VMEM((8, 64, width), bf16), dma((36,)), dma((8,))),
        (smem, hbm, hbm),
        (anywhere, vmem),
    )

    turned = lax.all_to_all(turned, PLANE, 0, 0, tiled=True)

    own = lax.all_gather(own, "zh", axis=0, tiled=True)
    own, turned, cached = lax.optimization_barrier((own, turned, cache[0]))
    states = called(repeat_kernel, shaped(bf16, 4, 128, width), (own,), 0, 1 << 20)
    states, sent_q, sent_o = lax.optimization_barrier((states, q0, o0))
    pair = called(pair_kernel, shaped(bf16, 2, R, 256), (sent_q, sent_o), 0, 1 << 16)
    states = lax.all_to_all(states, "x", 0, 0, tiled=True)

    p2 = swapped(pair, QUAD, 2)
    beside = swapped(cached, QUAD, 1)
    p1 = swapped(pair, QUAD, 1)
    lengths = prefix_len.reshape(1, R)
    first = called(
        first_prefix_kernel,
        shaped(f32, 3, 2, R),
        (place, lengths, far(cache[0]), far(q0), far(o0)),
        2 * 2 * 2 * R * POSITIONS * HEAD,
        1 << 20,
        (),
        (smem,),
        limit=16,
    )
    states, first = lax.optimization_barrier((states, first))

    states = states.reshape(R, width)
    heads = turned.reshape(2, 256, width)
    partial = called(
        project_kernel,
        shaped(f32, 8, TOKENS, 256),
        (states, heads),
        2 * R * 512 * width,
        3 << 20,
    )
    p2, partial = lax.optimization_barrier((p2, partial))
    p3 = swapped(p2, QUAD, 1)
    sources = (q0, o0, p1, p2, p3)
    before = called(
        prefix_kernel,
        shaped(f32, 3, 4, R),
        (place, lengths, first, far(cache[0]), beside, far(q0), far(o0), p2),
        2 * 2 * 8 * R * POSITIONS * HEAD * 4,
        3 << 20,
        (),
        (smem,),
        limit=16,
    )
    partial = lax.all_to_all(partial.astype(jnp.float16), PLANE, 0, 0, tiled=True)
    kv = (jnp.sum(partial.astype(f32), axis=0) * (1 / SPREAD)).astype(bf16)

    starts = doc_start.reshape(1, R)
    stats, pairs = called(
        new_stats_kernel,
        (shaped(f32, 3, 8, R), shaped(bf16, 4, 2, R, 256)),
        (place, starts, before, kv, *(far(source) for source in sources)),
        2 * 2 * 8 * R * TOKENS * HEAD * 4,
        3 << 20,
        (dma((8,)),),
        (smem, vmem, vmem, vmem) + (hbm,) * 5,
    )
    every = lax.all_gather(stats, QUAD, axis=0)
    grads = called(
        new_grads_kernel,
        shaped(bf16, TOKENS, 256),
        (place, kv, pairs, starts, every),
        4 * 2 * 8 * R * TOKENS * HEAD * 4,
        3 << 20,
        (
            pltpu.VMEM((3, 8, R), f32),
            pltpu.VMEM((TOKENS, HEAD), f32),
            pltpu.VMEM((TOKENS, HEAD), f32),
        ),
        (smem,),
    )
    kv_grads = lax.all_gather(grads, PLANE, axis=0, tiled=True).reshape(2, R, 256)

    hidden_part = called(
        hidden_kernel,
        shaped(bf16, 4, TOKENS, width),
        (kv_grads, heads),
        2 * R * 512 * width,
        3 << 20,
        (pltpu.VMEM((4, TOKENS, width), bf16), dma((4,))),
        outs=anywhere,
    )
    hidden_part, kv_grads = lax.optimization_barrier((hidden_part, kv_grads))
    over_x = lax.all_to_all(hidden_part, "x", 0, 0, tiled=True)
    over_x = called(
        reduce_x_kernel,
        shaped(bf16, 16, 32, width // 4),
        (over_x,),
        0,
        1 << 20,
        (pltpu.VMEM((16, 32, width // 4), bf16), dma((4,))),
        outs=anywhere,
    )

    mine, one, three = called(
        weight_kernel,
        (shaped(bf16, 2, 64, width),) + (shaped(bf16, 2, 96, width),) * 2,
        (member, kv_grads, states),
        2 * R * 512 * width,
        3 << 20,
        (pltpu.VMEM((512, width), bf16),),
        (smem,),
    )
    one = swapped(one, PLANE, 2)
    three = swapped(three, PLANE, 6)
    over_x, one = lax.optimization_barrier((over_x, one))
    over_z = lax.all_to_all(over_x, ("zh", "zl"), 0, 0, tiled=True)
    hidden_grads = jnp.sum(over_z.astype(f32), axis=0)

    upper = swapped(one[:, 64:], PLANE, 6)
    lower = swapped(three[:, 64:], PLANE, 2)
    kept, passed = called(
        cores_kernel,
        (shaped(bf16, 4, 64, width),) * 2,
        (member, mine, one, three, upper, lower),
        0,
        1 << 20,
        (),
        (smem,),
    )
    taken = swapped(passed, PLANE, 1)
    weight_grads = called(
        place_kernel,
        shaped(f32, 1, 64, 8 * width),
        (member, kept, taken),
        0,
        3 << 20,
        (),
        (smem,),
    )
    return hidden_grads, weight_grads


def solution(mesh):
    axes = ("zh", "x", "zl", "yh", "yl", "core")
    split = Mesh(mesh.devices.reshape(4, 4, 4, 2, 2, 2), axes)
    pipe = ("zh", "x")
    tensor = ("zl", "yh", "yl", "core")
    return jax.shard_map(
        shards,
        mesh=split,
        in_specs=(
            P(pipe, None),
            P(pipe, tensor, None),
            P(pipe, None, tensor),
            P(pipe, None, tensor),
            P(pipe, None, tensor, None),
            P(),
            P(),
        ),
        out_specs=(P(pipe, tensor), P(pipe, tensor, None)),
        check_vma=False,
    )
```
